256 devices in a mesh: ens: 4 (over y_hi, core), slab: 64 (over y_lo, z, x).
Axes of the slice: x: 4, y: 4 (y_hi: 2, y_lo: 2; y = y_hi * 2 + y_lo), z: 8, core: 2. Of those that a mesh axis runs over, the one named last changes fastest.
Arguments:
- tracer: float32 [32, 1024, 4096], P('ens', 'slab'), may hold values from -6 to 6
- coefficients: float32 [4, 1024, 4096], P(None, 'slab'), may hold values from -1.5 to 1.5, as said below
- parameters: float32 [32, 4096], P('ens'), may hold values from -6 to 6
- obs_index: int32 [131072], P('slab'), may hold values from 0 to 65535, as said below
- obs_values: float32 [32, 131072], P('ens', 'slab'), may hold values from -6 to 6
- obs_variance: float32 [131072], P('slab'), may hold values from 0.1 to 1
- member_group: int32 [32], replicated, may hold values from 0 to 7, as said below
Outputs:
- final_field: float32 [32, 1024, 4096], P('ens', 'slab')
- updated_params: float32 [32, 4096], P('ens')
The draws below stay inside these ranges and needn't reach their ends.
Inputs may be any that keep to these rules, and one draw needn't show every extreme that they name: `obs_index`: every slab has an observation at flat index 0 and one at 65535; indices may repeat. `member_group`: every group holds exactly 4 members. `coefficients`: the Courant numbers lie within -0.3 to 0.3, the diffusion number within 0.02 to 0.1.
All inputs are finite; a program needn't handle non-finite values.
Results may differ from the reference program's by a relative error of at most 0.0003.
Values sent between devices are 32-bit elements; how exact they have to be, the bound alone decides.
A program may use at most 128 MiB of HBM per device.

```python
import math
import jax
import jax.numpy as jnp
from jax import lax

P_SIZE = 4096
CX = 16
OBS_DEV = 2048
STEPS = 4
GROUPS = 8
MEMBERS = 32
NX = 1024
NOBS = 131072
N_SLAB = 64


def draw_coefficients(key, part):
    subkeys = jax.random.split(key, 4)
    grid_shape = (NX, P_SIZE)
    speed_x = jax.random.uniform(subkeys[0], grid_shape, minval=-0.3, maxval=0.3)
    speed_y = jax.random.uniform(subkeys[1], grid_shape, minval=-0.3, maxval=0.3)
    diffusion = jnp.exp(jax.random.uniform(subkeys[2], grid_shape, minval=math.log(0.02), maxval=math.log(0.1)))
    pattern = 0.5 * jax.random.truncated_normal(subkeys[3], -3.0, 3.0, grid_shape)
    return jnp.stack([speed_x, speed_y, diffusion, pattern]).astype(jnp.float32)


def draw_obs_index(key, part):
    blocks = NOBS // OBS_DEV
    values = jax.random.randint(key, (blocks, OBS_DEV), 0, CX * P_SIZE, dtype=jnp.int32)
    values = values.at[:, 0].set(CX * P_SIZE - 1).at[:, 1].set(0)
    return values.reshape(NOBS)


def draw_member_group(key, part):
    shuffled = jax.random.permutation(key, MEMBERS)
    return (shuffled % GROUPS).astype(jnp.int32)


def block_scale(own_key, dims, cuts, smallest, top_value):
    gain, own = 1.0, jax.random.fold_in(own_key, 6)
    for dim, blocks in cuts:
        draws = jnp.exp(jax.random.uniform(jax.random.fold_in(own, dim), (blocks,), jnp.float32, smallest / len(cuts), top_value / len(cuts)))
        gain = gain * jnp.repeat(draws, dims[dim] // blocks).reshape([-1 if axis == dim else 1 for axis in range(len(dims))])
    return gain


def scatter_about(rng, extent, scale, reach, shards=(), kind=jnp.bfloat16):
    drawn = scale * jax.random.normal(rng, extent, jnp.float32)
    if shards:
        drawn = drawn * block_scale(rng, extent, shards, -0.22, 0.18)
    return jnp.clip(drawn, -reach, reach).astype(kind)


def setup_inputs(seed: int = 0) -> dict:
    streams_of = jax.random.split(jax.random.key(seed), 8)
    return {
        "tracer": scatter_about(streams_of[0], (MEMBERS, NX, P_SIZE), 1.0, 6.0, ((0, 4), (1, 64)), jnp.float32),
        "coefficients": draw_coefficients(jax.random.fold_in(streams_of[7], 71), 0),
        "parameters": scatter_about(streams_of[2], (MEMBERS, P_SIZE), 1.0, 6.0, ((0, 4),), jnp.float32),
        "obs_index": draw_obs_index(jax.random.fold_in(streams_of[7], 71), 0),
        "obs_values": scatter_about(streams_of[4], (MEMBERS, NOBS), 1.0, 6.0, ((0, 4), (1, 64)), jnp.float32),
        "obs_variance": jnp.clip(jnp.exp(math.log(1.0) - 2.3025851 * jax.random.uniform(streams_of[5], (NOBS,), jnp.float32) ** block_scale(streams_of[5], (NOBS,), ((0, 64),), -0.2, 0.2)), 0.1, 1.0),
        "member_group": draw_member_group(jax.random.fold_in(streams_of[7], 71), 0),
    }


def hdot(left, right):
    return jnp.dot(left.astype(jnp.float32), right.astype(jnp.float32), precision=lax.Precision.HIGHEST, preferred_element_type=jnp.float32)

def minmod(left, right):
    return jnp.where(left * right > 0.0, jnp.where(jnp.abs(left) < jnp.abs(right), left, right), 0.0)

def upwind(minus_two, minus_one, centre, plus_one, plus_two, speed):
    slope_back = minmod(minus_one - minus_two, centre - minus_one)
    slope_here = minmod(centre - minus_one, plus_one - centre)
    slope_next = minmod(plus_one - centre, plus_two - plus_one)
    forward = centre + 0.5 * slope_here - (minus_one + 0.5 * slope_back)
    backward = plus_one - 0.5 * slope_next - (centre - 0.5 * slope_here)
    return speed * jnp.where(speed > 0.0, forward, backward)

def advance(padded, coefficients, params):
    out_rows = padded.shape[-2] - 4
    along_x = [lax.slice_in_dim(padded, offset, offset + out_rows, axis=padded.ndim - 2) for offset in range(5)]
    centre = along_x[2]
    along_y = [jnp.roll(centre, shift, axis=-1) for shift in (2, 1, 0, -1, -2)]
    advection = upwind(*along_x, coefficients[0]) + upwind(*along_y, coefficients[1])
    laplace = along_x[1] + along_x[3] + along_y[1] + along_y[3] - 4.0 * centre
    source = jnp.expand_dims(params, -2) * coefficients[3]
    return centre - advection + coefficients[2] * laplace + source

def reference(tracer, coefficients, parameters, obs_index, obs_values, obs_variance, member_group):

    def one_member(item):
        field_now, row_params = item
        for step_index in range(STEPS):
            field_now = advance(jnp.pad(field_now, ((2, 2), (0, 0))), coefficients, row_params)
        return field_now
    final_field = lax.map(one_member, (tracer, parameters))
    flat_state = final_field.reshape(MEMBERS, N_SLAB, CX * P_SIZE)
    where_obs = jnp.broadcast_to(obs_index.reshape(1, N_SLAB, OBS_DEV), (MEMBERS, N_SLAB, OBS_DEV))
    predicted = jnp.take_along_axis(flat_state, where_obs, axis=2).reshape(MEMBERS, NOBS)
    weight = 1.0 / (obs_variance * NOBS)
    innovation = (obs_values - predicted) * weight[None, :]
    same_group = (member_group[:, None] == member_group[None, :]).astype(jnp.float32)
    per_group = MEMBERS // GROUPS
    spread = 1.0 / math.sqrt(per_group - 1)
    anomalies = (predicted - hdot(same_group, predicted) / per_group) * spread
    gram = hdot(anomalies * weight[None, :], anomalies.T)
    mixed = hdot(anomalies, innovation.T)
    system = jnp.eye(MEMBERS, dtype=jnp.float32) + same_group * gram
    factor = jnp.linalg.cholesky(system)
    solved = jax.scipy.linalg.solve_triangular(factor, same_group * mixed, lower=True)
    solved = jax.scipy.linalg.solve_triangular(factor.T, solved, lower=False)
    param_anomalies = (parameters - hdot(same_group, parameters) / per_group) * spread
    updated_params = parameters + hdot(solved.T, param_anomalies)
    return (final_field, updated_params)
```

```python
import functools
import math

import jax
import jax.numpy as jnp
from jax import lax
from jax.experimental import pallas as pl
from jax.experimental.pallas import tpu as pltpu
from jax.sharding import PartitionSpec as P

STEPS = 4
GROUPS = 8
LANES = 128
CHUNKS = 4
NEAR = 4
MESH = pl.DeviceIdType.MESH
F32 = jnp.float32
PAIRS = [(a, b) for a in range(4) for b in range(a, 4)]


def lanes_of():
    return lax.broadcasted_iota(jnp.int32, (8, LANES), 1)


def sublanes_of():
    return lax.broadcasted_iota(jnp.int32, (8, LANES), 0)


def half_minmod(left, right):
    return 0.5 * jnp.maximum(jnp.minimum(left, right), jnp.minimum(jnp.maximum(left, right), 0.0))


def across_rows(rows, speeds, spreads, bases):
    count = len(rows) - 4
    diffs = [rows[i + 1] - rows[i] for i in range(count + 3)]
    halves = [half_minmod(diffs[i], diffs[i + 1]) for i in range(count + 2)]
    upper = [rows[i + 1] + halves[i] for i in range(count + 2)]
    lower = [rows[i + 1] - halves[i] for i in range(count + 2)]
    out = []
    for i in range(count):
        speed = speeds[i]
        change = jnp.where(speed > 0.0, upper[i + 1] - upper[i], lower[i + 2] - lower[i + 1])
        out.append(bases[i] - speed * change + spreads[i] * (diffs[i + 2] - diffs[i + 1]))
    return out


def kernel(
    slabs,
    tiles,
    group_ref,
    index_ref,
    tracer_ref,
    coef_ref,
    params_ref,
    values_ref,
    variance_ref,
    field_out,
    params_out,
    tracer_v,
    coef_v,
    own_params,
    variance_v,
    cells,
    halo,
    speed_x,
    speed_y,
    spread,
    source,
    partial_c,
    final_c,
    field_v,
    all_params,
    all_values,
    picked,
    all_picked,
    moved,
    part_near,
    part_far,
    sums_near,
    sums_far,
    load_sem,
    out_sem,
    halo_send,
    halo_recv,
    ens_send,
    ens_recv,
    near_send,
    near_recv,
    far_send,
    far_recv,
):
    ens = lax.axis_index("ens")
    slab = lax.axis_index("slab")
    rows = 16
    per_chunk = tiles // CHUNKS
    far_count = slabs // NEAR
    near_count = 4 * NEAR
    obs_tiles = picked.shape[0]
    quarter = obs_tiles // 4
    has_left = slab > 0
    has_right = slab < slabs - 1
    near_me = ens * NEAR + lax.rem(slab, NEAR)
    far_me = slab // NEAR
    lane = lanes_of()
    first_lane = lane == 0
    last_lane = lane == LANES - 1

    def near_device(i):
        return (i // NEAR, far_me * NEAR + lax.rem(i, NEAR))

    def far_device(i):
        return (ens, i * NEAR + lax.rem(slab, NEAR))

    loads = [
        pltpu.make_async_copy(tracer_ref, tracer_v, load_sem.at[0]),
        pltpu.make_async_copy(coef_ref, coef_v, load_sem.at[1]),
        pltpu.make_async_copy(params_ref, own_params, load_sem.at[2]),
        pltpu.make_async_copy(variance_ref, variance_v, load_sem.at[3]),
        pltpu.make_async_copy(
            values_ref.at[:, pl.ds(pl.multiple_of(ens * (quarter * LANES), LANES), quarter * LANES)],
            all_values.at[ens],
            load_sem.at[4],
        ),
    ]
    for load in loads:
        load.start()

    barrier = pltpu.get_barrier_semaphore()

    @pl.loop(1, near_count)
    def _(p):
        pl.semaphore_signal(
            barrier, inc=1, device_id=near_device(lax.rem(near_me + p, near_count)), device_id_type=MESH
        )

    @pl.loop(1, far_count)
    def _(p):
        pl.semaphore_signal(
            barrier, inc=1, device_id=far_device(lax.rem(far_me + p, far_count)), device_id_type=MESH
        )

    @pl.when(has_left)
    def _():
        pl.semaphore_signal(barrier, inc=1, device_id=(ens, slab - 1), device_id_type=MESH)

    @pl.when(has_right)
    def _():
        pl.semaphore_signal(barrier, inc=1, device_id=(ens, slab + 1), device_id_type=MESH)

    loads[0].wait()

    def of_tile(row, j):
        return (row // 8 * tiles + j) * 8 + row % 8

    def take_row(row):
        for j in range(tiles):
            cells[0, row, j] = tracer_v[pl.ds(of_tile(row, j), 8, stride=rows * tiles), :]

    take_row(0)
    take_row(1)
    take_row(rows - 2)
    take_row(rows - 1)

    zero = jnp.zeros((8, LANES), F32)

    def clear(side):
        @pl.loop(0, STEPS)
        def _(t):
            for r in range(2):
                for j in range(tiles):
                    halo[t, side, r, j] = zero

    pl.when(jnp.logical_not(has_left))(functools.partial(clear, 0))
    pl.when(jnp.logical_not(has_right))(functools.partial(clear, 1))

    neighbours = jnp.where(has_left, 1, 0) + jnp.where(has_right, 1, 0)
    pl.semaphore_wait(barrier, near_count + far_count - 2 + neighbours)

    def halo_copy(t, side, k):
        window = pl.ds(k * per_chunk, per_chunk)
        return pltpu.make_async_remote_copy(
            src_ref=cells.at[t, pl.ds(rows - 2, 2) if side == 0 else pl.ds(0, 2), window],
            dst_ref=halo.at[t, side, :, window],
            send_sem=halo_send.at[t, side, k],
            recv_sem=halo_recv.at[t, side, k],
            device_id=(ens, slab + 1 if side == 0 else slab - 1),
            device_id_type=MESH,
        )

    def send_halo(t, side, k):
        @pl.when(has_right if side == 0 else has_left)
        def _():
            halo_copy(t, side, k).start()

    def wait_halo(t, side, k):
        @pl.when(has_left if side == 0 else has_right)
        def _():
            halo_copy(t, side, k).wait_recv()

    @pl.loop(0, CHUNKS)
    def _(k):
        send_halo(0, 0, k)
        send_halo(0, 1, k)

    loads[2].wait()

    def params_copy(p):
        return pltpu.make_async_remote_copy(
            src_ref=own_params,
            dst_ref=all_params.at[ens],
            send_sem=ens_send.at[0, p],
            recv_sem=ens_recv.at[0, p],
            device_id=(lax.rem(ens + p, 4), slab),
            device_id_type=MESH,
        )

    def values_copy(p):
        target = lax.rem(ens + p, 4)
        return pltpu.make_async_remote_copy(
            src_ref=values_ref.at[:, pl.ds(pl.multiple_of(target * (quarter * LANES), LANES), quarter * LANES)],
            dst_ref=all_values.at[ens],
            send_sem=ens_send.at[1, p],
            recv_sem=ens_recv.at[1, p],
            device_id=(target, slab),
            device_id_type=MESH,
        )

    def picked_copy(p):
        target = lax.rem(ens + p, 4)
        return pltpu.make_async_remote_copy(
            src_ref=picked.at[pl.ds(target * quarter, quarter)],
            dst_ref=all_picked.at[ens],
            send_sem=ens_send.at[2, p],
            recv_sem=ens_recv.at[2, p],
            device_id=(target, slab),
            device_id_type=MESH,
        )

    for p in range(1, 4):
        params_copy(p).start()
        values_copy(p).start()

    for row in range(2, rows - 2):
        take_row(row)

    loads[1].wait()

    @pl.loop(0, tiles)
    def _(j):
        window = pl.ds(pl.multiple_of(j * LANES, LANES), LANES)
        for r in range(rows):
            expanded = [
                jnp.broadcast_to(coef_v[c, pl.ds(r, 1), window], (8, LANES)) for c in range(4)
            ]
            speed_x[r, j] = expanded[0]
            speed_y[r, j] = expanded[1]
            spread[r, j] = expanded[2]
            source[r, j] = own_params[:, window] * expanded[3]

    def from_left(here, before):
        return jnp.where(first_lane, pltpu.roll(before, 1, 1), pltpu.roll(here, 1, 1))

    def from_right(here, after):
        return jnp.where(last_lane, pltpu.roll(after, LANES - 1, 1), pltpu.roll(here, LANES - 1, 1))

    def along_columns(t, r, k):
        start = k * per_chunk
        n = per_chunk
        at = (
            [lax.rem(start + tiles - 1, tiles)]
            + [start + i for i in range(n)]
            + [lax.rem(start + n, tiles)]
        )
        here = [cells[t, r, i] for i in at]
        turned = [pltpu.roll(c, LANES - 1, 1) for c in here]
        diffs = [
            (jnp.where(last_lane, turned[i + 1], turned[i]) if i <= n else turned[i]) - here[i]
            for i in range(n + 2)
        ]
        turned = [pltpu.roll(d, 1, 1) for d in diffs]
        earlier = [
            jnp.where(first_lane, turned[i - 1], turned[i]) if i > 0 else turned[i]
            for i in range(n + 2)
        ]
        halves = [half_minmod(earlier[i], diffs[i]) for i in range(n + 2)]
        upper = [here[i] + halves[i] for i in range(n + 1)]
        lower = [None] + [here[i] - halves[i] for i in range(1, n + 2)]
        upper_turned = [pltpu.roll(u, 1, 1) for u in upper]
        lower_turned = [None] + [pltpu.roll(v, LANES - 1, 1) for v in lower[1:]]
        for i in range(1, n + 1):
            forward = upper[i] - jnp.where(first_lane, upper_turned[i - 1], upper_turned[i])
            backward = jnp.where(last_lane, lower_turned[i + 1], lower_turned[i]) - lower[i]
            speed = speed_y[r, at[i]]
            change = jnp.where(speed > 0.0, forward, backward)
            partial_c[r, at[i]] = (
                here[i]
                - speed * change
                + spread[r, at[i]] * (diffs[i] - earlier[i])
                + source[r, at[i]]
            )

    def finish_rows(t, first, last, j, before, after, store):
        taken = before + [cells[t, r, j] for r in range(max(first - 2, 0), min(last + 2, rows))] + after
        new = across_rows(
            taken,
            [speed_x[r, j] for r in range(first, last)],
            [spread[r, j] for r in range(first, last)],
            [partial_c[r, j] for r in range(first, last)],
        )
        for r, value in zip(range(first, last), new):
            store(r, j, value)

    def one_step(t, final):
        def store(r, j, value):
            if final:
                final_c[r * tiles + j] = value
                field_v[pl.ds(of_tile(r, j), 8, stride=rows * tiles), :] = value
            else:
                cells[t + 1, r, j] = value

        @pl.loop(0, CHUNKS)
        def _(k):
            for r in (0, 1, rows - 2, rows - 1):
                along_columns(t, r, k)

        @pl.loop(0, CHUNKS)
        def _(k):
            wait_halo(t, 0, k)

            @pl.loop(0, per_chunk)
            def _(i):
                j = k * per_chunk + i
                finish_rows(t, 0, 2, j, [halo[t, 0, 0, j], halo[t, 0, 1, j]], [], store)

            if not final:
                send_halo(t + 1, 1, k)
            wait_halo(t, 1, k)

            @pl.loop(0, per_chunk)
            def _(i):
                j = k * per_chunk + i
                finish_rows(t, rows - 2, rows, j, [], [halo[t, 1, 0, j], halo[t, 1, 1, j]], store)

            if not final:
                send_halo(t + 1, 0, k)

            @pl.loop(2, rows - 2, step=2)
            def _(r):
                along_columns(t, r, k)
                along_columns(t, r + 1, k)

            @pl.loop(0, per_chunk)
            def _(i):
                finish_rows(t, 2, rows - 2, k * per_chunk + i, [], [], store)

    @pl.loop(0, STEPS - 1)
    def _(t):
        one_step(t, False)

    members = 32
    group_row = jnp.zeros((8, LANES), jnp.int32) - 1
    for m in range(members):
        group_row = jnp.where(lane == m, group_ref[m], group_row)
    slot_row = jnp.zeros((8, LANES), jnp.int32)
    for m in range(members):
        slot_row = slot_row + jnp.where((group_row == group_ref[m]) & (lane > m), 1, 0)
    sub = sublanes_of()
    group_own = jnp.zeros((8, LANES), jnp.int32)
    for i in range(8):
        group_own = jnp.where(sub == i, group_ref[ens * 8 + i], group_own)
    slot_own = jnp.zeros((8, LANES), jnp.int32)
    for m in range(members):
        slot_own = slot_own + jnp.where((group_own == group_ref[m]) & (sub + ens * 8 > m), 1, 0)
    in_slot = [jnp.where(slot_row == s, 1.0, 0.0) for s in range(4)]
    by_group = jnp.concatenate(
        [jnp.where(group_row == sub, in_slot[s], 0.0) for s in range(4)], axis=0
    )[:, :members]
    by_own = jnp.concatenate(
        [jnp.where(group_row == group_own, in_slot[s], 0.0) for s in range(4)], axis=0
    )[:, :members]

    def pick(chosen, held):
        return jnp.dot(chosen, held, precision=lax.Precision.HIGHEST, preferred_element_type=F32)

    spread_of = 1.0 / math.sqrt(3.0)

    def centred(four):
        mean = (four[0] + four[1] + four[2] + four[3]) * 0.25
        return [(x - mean) * spread_of for x in four]

    all_params[ens] = own_params[...]
    for p in range(1, 4):
        params_copy(p).wait_recv()
    columns = tiles * LANES
    piece = min(512, columns)

    @pl.loop(0, columns // piece)
    def _(c):
        window = pl.ds(pl.multiple_of(c * piece, piece), piece)
        held = jnp.concatenate([all_params[q, :, window] for q in range(4)], axis=0)
        ordered = pick(by_own, held)
        for s, value in enumerate(centred([ordered[s * 8 : s * 8 + 8] for s in range(4)])):
            moved[s, :, window] = value

    loads[3].wait()
    loads[4].wait()
    for p in range(1, 4):
        values_copy(p).wait_recv()
    ordered_values = pick(by_group, jnp.concatenate([all_values[q] for q in range(4)], axis=0))
    total_obs = float(obs_tiles * LANES * slabs)
    weights = [
        jnp.broadcast_to(1.0 / (variance_v[pl.ds(ens * quarter + i, 1), :] * total_obs), (8, LANES))
        for i in range(quarter)
    ]
    weight = jnp.concatenate(weights, axis=1)

    one_step(STEPS - 1, True)

    field_store = pltpu.make_async_copy(field_v, field_out, out_sem)
    field_store.start()

    def gather_quarter(q):
        @pl.loop(0, quarter)
        def _(i):
            tile = q * quarter + i

            def some(b, taken):
                for u in range(16):
                    at = b * 16 + u
                    where = index_ref[tile * LANES + at]
                    found = pltpu.roll(final_c[where >> 7], (at - where) & (LANES - 1), 1)
                    taken = jnp.where(lane == at, found, taken)
                return taken

            picked[tile] = lax.fori_loop(0, LANES // 16, some, jnp.zeros((8, LANES), F32))

    for p in range(1, 4):
        gather_quarter(lax.rem(ens + p, 4))
        picked_copy(p).start()
    gather_quarter(ens)
    for i in range(quarter):
        all_picked[ens, i] = picked[ens * quarter + i]
    for p in range(1, 4):
        picked_copy(p).wait_recv()

    held = jnp.concatenate(
        [
            jnp.concatenate([all_picked[q, i] for i in range(quarter)], axis=1)
            for q in range(4)
        ],
        axis=0,
    )
    ordered = pick(by_group, held)
    ordered = [ordered[s * 8 : s * 8 + 8] for s in range(4)]
    innovation = [
        (ordered_values[s * 8 : s * 8 + 8] - ordered[s]) * weight for s in range(4)
    ]
    anomalies = centred(ordered)
    weighted = [a * weight for a in anomalies]
    products = [(weighted[a], anomalies[b]) for a, b in PAIRS] + [
        (anomalies[a], innovation[b]) for a in range(4) for b in range(4)
    ]
    packed = jnp.zeros((8, LANES), F32)
    for position, (left, right) in enumerate(products):
        both = left * right
        folded = both[:, :LANES]
        for i in range(1, quarter):
            folded = folded + both[:, i * LANES : (i + 1) * LANES]
        packed = jnp.where(lane == position, jnp.sum(folded, axis=1, keepdims=True), packed)

    def sum_over(value, part, sums, me, count, device, send, recv):
        part[...] = value

        def copy(i, slot):
            return pltpu.make_async_remote_copy(
                src_ref=part,
                dst_ref=sums.at[me],
                send_sem=send.at[slot],
                recv_sem=recv.at[slot],
                device_id=device(i),
                device_id_type=MESH,
            )

        @pl.loop(1, count)
        def _(p):
            copy(lax.rem(me + p, count), p).start()

        sums[me] = value

        @pl.loop(1, count)
        def _(p):
            copy(lax.rem(me + p, count), p).wait()

        total = sums[0]
        for i in range(1, count):
            total = total + sums[i]
        return total

    total = sum_over(packed, part_near, sums_near, near_me, near_count, near_device, near_send, near_recv)
    total = sum_over(total, part_far, sums_far, far_me, far_count, far_device, far_send, far_recv)

    mine = jnp.zeros((8, LANES), F32)
    for g in range(GROUPS):
        mine = jnp.where(group_own == g, jnp.broadcast_to(total[g : g + 1], (8, LANES)), mine)

    def column(i):
        return jnp.broadcast_to(mine[:, i : i + 1], (8, LANES))

    a = {}
    for i, (p, q) in enumerate(PAIRS):
        a[p, q] = column(i) + (1.0 if p == q else 0.0)
    b = []
    for p in range(4):
        value = column(len(PAIRS) + p * 4)
        for q in range(1, 4):
            value = jnp.where(slot_own == q, column(len(PAIRS) + p * 4 + q), value)
        b.append(value)
    low = {}
    for p in range(4):
        for q in range(p + 1, 4):
            low[q, p] = a[p, q] / a[p, p]
        for q in range(p + 1, 4):
            for r in range(q, 4):
                a[q, r] = a[q, r] - low[q, p] * a[p, r]
    for p in range(4):
        for q in range(p + 1, 4):
            b[q] = b[q] - low[q, p] * b[p]
    solved = [b[p] / a[p, p] for p in range(4)]
    for p in range(2, -1, -1):
        for q in range(p + 1, 4):
            solved[p] = solved[p] - low[q, p] * solved[q]

    for j in range(tiles):
        window = pl.ds(j * LANES, LANES)
        value = own_params[:, window]
        for s in range(4):
            value = value + solved[s] * moved[s, :, window]
        params_out[:, window] = value

    for p in range(1, 4):
        params_copy(p).wait_send()
        values_copy(p).wait_send()
        picked_copy(p).wait_send()

    @pl.loop(0, STEPS)
    def _(t):
        @pl.loop(0, CHUNKS)
        def _(k):
            @pl.when(has_right)
            def _():
                halo_copy(t, 0, k).wait_send()

            @pl.when(has_left)
            def _():
                halo_copy(t, 1, k).wait_send()

    field_store.wait()


def local(tracer, coefficients, parameters, obs_index, obs_values, obs_variance, member_group):
    members, rows, columns = tracer.shape
    slabs = lax.axis_size("slab")
    tiles = columns // LANES
    obs_tiles = obs_index.shape[0] // LANES
    far_count = slabs // NEAR
    near_count = 4 * NEAR
    grid = (rows, tiles, 8, LANES)
    smem = pl.BlockSpec(memory_space=pltpu.SMEM)
    anywhere = pl.BlockSpec(memory_space=pl.ANY)
    vmem = pl.BlockSpec(memory_space=pltpu.VMEM)
    field, params = pl.pallas_call(
        functools.partial(kernel, slabs, tiles),
        out_shape=(
            jax.ShapeDtypeStruct((members * rows * tiles, LANES), F32),
            jax.ShapeDtypeStruct((members, columns), F32),
        ),
        in_specs=[smem, smem, anywhere, anywhere, anywhere, anywhere, anywhere],
        out_specs=(anywhere, vmem),
        scratch_shapes=[
            pltpu.VMEM((members * rows * tiles, LANES), F32),
            pltpu.VMEM((4, rows, columns), F32),
            pltpu.VMEM((members, columns), F32),
            pltpu.VMEM((obs_tiles, LANES), F32),
            pltpu.VMEM((STEPS,) + grid, F32),
            pltpu.VMEM((STEPS, 2, 2) + grid[1:], F32),
            pltpu.VMEM(grid, F32),
            pltpu.VMEM(grid, F32),
            pltpu.VMEM(grid, F32),
            pltpu.VMEM(grid, F32),
            pltpu.VMEM(grid, F32),
            pltpu.VMEM((rows * tiles, 8, LANES), F32),
            pltpu.VMEM((members * rows * tiles, LANES), F32),
            pltpu.VMEM((4, members, columns), F32),
            pltpu.VMEM((4, members, obs_tiles // 4 * LANES), F32),
            pltpu.VMEM((obs_tiles, 8, LANES), F32),
            pltpu.VMEM((4, obs_tiles // 4, 8, LANES), F32),
            pltpu.VMEM((4, members, columns), F32),
            pltpu.VMEM((8, LANES), F32),
            pltpu.VMEM((8, LANES), F32),
            pltpu.VMEM((near_count, 8, LANES), F32),
            pltpu.VMEM((far_count, 8, LANES), F32),
            pltpu.SemaphoreType.DMA((5,)),
            pltpu.SemaphoreType.DMA,
            pltpu.SemaphoreType.DMA((STEPS, 2, CHUNKS)),
            pltpu.SemaphoreType.DMA((STEPS, 2, CHUNKS)),
            pltpu.SemaphoreType.DMA((3, 4)),
            pltpu.SemaphoreType.DMA((3, 4)),
            pltpu.SemaphoreType.DMA((near_count,)),
            pltpu.SemaphoreType.DMA((near_count,)),
            pltpu.SemaphoreType.DMA((far_count,)),
            pltpu.SemaphoreType.DMA((far_count,)),
        ],
        compiler_params=pltpu.CompilerParams(
            collective_id=0, has_side_effects=True, vmem_limit_bytes=56 * 1024 * 1024
        ),
    )(
        member_group,
        obs_index,
        tracer.reshape(members, rows // 8, 8, tiles, LANES).transpose(0, 1, 3, 2, 4).reshape(-1, LANES),
        coefficients,
        parameters,
        obs_values,
        obs_variance.reshape(obs_tiles, LANES),
    )
    field = field.reshape(members, rows // 8, tiles, 8, LANES).transpose(0, 1, 3, 2, 4)
    return field.reshape(members, rows, columns), params


def solution(mesh):
    in_specs = (
        P("ens", "slab", None),
        P(None, "slab", None),
        P("ens", None),
        P("slab"),
        P("ens", "slab"),
        P("slab"),
        P(),
    )
    out_specs = (P("ens", "slab", None), P("ens", None))
    return jax.shard_map(local, mesh=mesh, in_specs=in_specs, out_specs=out_specs, check_vma=False)
```

```python
import functools
import math

import jax
import jax.numpy as jnp
from jax import lax
from jax.experimental import pallas as pl
from jax.experimental.pallas import tpu as pltpu
from jax.sharding import PartitionSpec as P

STEPS = 4
GROUPS = 8
LANES = 128
CHUNKS = 4
NEAR = 4
BLOCKS = 16
EDGE = 8
MESH = pl.DeviceIdType.MESH
F32 = jnp.float32
PAIRS = [(a, b) for a in range(4) for b in range(a, 4)]


def lanes_of():
    return lax.broadcasted_iota(jnp.int32, (8, LANES), 1)


def sublanes_of():
    return lax.broadcasted_iota(jnp.int32, (8, LANES), 0)


def parts_of(value):
    high = value.astype(jnp.bfloat16)
    rest = value - high.astype(F32)
    middle = rest.astype(jnp.bfloat16)
    low = (rest - middle.astype(F32)).astype(jnp.bfloat16)
    return jnp.concatenate([high, middle, low], axis=1)


def half_minmod(left, right):
    return 0.5 * jnp.maximum(jnp.minimum(left, right), jnp.minimum(jnp.maximum(left, right), 0.0))


def across_rows(rows, speeds, spreads, bases):
    count = len(rows) - 4
    diffs = [rows[i + 1] - rows[i] for i in range(count + 3)]
    halves = [half_minmod(diffs[i], diffs[i + 1]) for i in range(count + 2)]
    upper = [rows[i + 1] + halves[i] for i in range(count + 2)]
    lower = [rows[i + 1] - halves[i] for i in range(count + 2)]
    out = []
    for i in range(count):
        speed = speeds[i]
        change = jnp.where(speed > 0.0, upper[i + 1] - upper[i], lower[i + 2] - lower[i + 1])
        out.append(bases[i] - speed * change + spreads[i] * (diffs[i + 2] - diffs[i + 1]))
    return out


def kernel(
    slabs,
    tiles,
    group_ref,
    index_ref,
    tracer_ref,
    coef_ref,
    params_ref,
    values_ref,
    variance_ref,
    field_out,
    params_out,
    tracer_v,
    coef_v,
    own_params,
    variance_v,
    index_v,
    place_v,
    place,
    spread_out,
    pick_out,
    params_t,
    coef_x,
    cells,
    halo,
    slopes,
    partial_c,
    final_c,
    mask_v,
    found,
    field_v,
    all_params,
    all_values,
    picked,
    all_picked,
    moved,
    part_near,
    part_far,
    sums_near,
    sums_far,
    load_sem,
    out_sem,
    halo_send,
    halo_recv,
    ens_send,
    ens_recv,
    near_send,
    near_recv,
    far_send,
    far_recv,
):
    ens = lax.axis_index("ens")
    slab = lax.axis_index("slab")
    rows = 16
    segment = tiles * LANES // BLOCKS
    halves = segment // LANES
    per_chunk = segment // CHUNKS
    groups = per_chunk // 8
    far_count = slabs // NEAR
    near_count = 4 * NEAR
    quarter = picked.shape[1]
    obs_tiles = 4 * quarter
    has_left = slab > 0
    has_right = slab < slabs - 1
    near_me = ens * NEAR + lax.rem(slab, NEAR)
    far_me = slab // NEAR
    lane = lanes_of()
    sub = sublanes_of()

    def near_device(i):
        return (i // NEAR, far_me * NEAR + lax.rem(i, NEAR))

    def far_device(i):
        return (ens, i * NEAR + lax.rem(slab, NEAR))

    loads = [
        pltpu.make_async_copy(tracer_ref, tracer_v, load_sem.at[0]),
        pltpu.make_async_copy(coef_ref, coef_v, load_sem.at[1]),
        pltpu.make_async_copy(params_ref, own_params, load_sem.at[2]),
        pltpu.make_async_copy(variance_ref, variance_v, load_sem.at[3]),
        pltpu.make_async_copy(
            values_ref.at[:, pl.ds(pl.multiple_of(ens * (quarter * LANES), LANES), quarter * LANES)],
            all_values.at[ens],
            load_sem.at[4],
        ),
        pltpu.make_async_copy(index_ref, index_v, load_sem.at[5]),
    ]
    for load in loads:
        load.start()

    barrier = pltpu.get_barrier_semaphore()

    @pl.loop(1, near_count)
    def _(p):
        pl.semaphore_signal(
            barrier, inc=1, device_id=near_device(lax.rem(near_me + p, near_count)), device_id_type=MESH
        )

    @pl.loop(1, far_count)
    def _(p):
        pl.semaphore_signal(
            barrier, inc=1, device_id=far_device(lax.rem(far_me + p, far_count)), device_id_type=MESH
        )

    @pl.when(has_left)
    def _():
        pl.semaphore_signal(barrier, inc=1, device_id=(ens, slab - 1), device_id_type=MESH)

    @pl.when(has_right)
    def _():
        pl.semaphore_signal(barrier, inc=1, device_id=(ens, slab + 1), device_id_type=MESH)

    loads[0].wait()

    def of_tile(row, j):
        return (row // 8 * tiles + j) * 8 + lax.rem(row, 8)

    def take_row(row):
        for h in range(halves):
            block = [
                tracer_v[pl.ds(of_tile(row, b * halves + h), 8, stride=rows * tiles), :]
                for b in range(BLOCKS)
            ]
            cells[0, row, pl.ds(EDGE + h * LANES, LANES), :] = jnp.transpose(jnp.concatenate(block, axis=0))

    def edge_row(i):
        return i + i // 2 * (rows - 4)

    @pl.loop(0, 4)
    def _(i):
        take_row(edge_row(i))

    zero = jnp.zeros((8, LANES), F32)

    def clear(side):
        @pl.loop(0, STEPS)
        def _(t):
            for r in range(2):
                for i in range(segment // 8):
                    halo[t, side, r, pl.ds(i * 8, 8), :] = zero

    pl.when(jnp.logical_not(has_left))(functools.partial(clear, 0))
    pl.when(jnp.logical_not(has_right))(functools.partial(clear, 1))

    neighbours = jnp.where(has_left, 1, 0) + jnp.where(has_right, 1, 0)
    pl.semaphore_wait(barrier, near_count + far_count - 2 + neighbours)

    def halo_copy(t, side, k):
        start = pl.multiple_of(k * per_chunk, per_chunk)
        return pltpu.make_async_remote_copy(
            src_ref=cells.at[
                t,
                pl.ds(rows - 2, 2) if side == 0 else pl.ds(0, 2),
                pl.ds(pl.multiple_of(EDGE + start, 8), per_chunk),
            ],
            dst_ref=halo.at[t, side, :, pl.ds(start, per_chunk)],
            send_sem=halo_send.at[t, side, k],
            recv_sem=halo_recv.at[t, side, k],
            device_id=(ens, slab + 1 if side == 0 else slab - 1),
            device_id_type=MESH,
        )

    def send_halo(t, side, k):
        @pl.when(has_right if side == 0 else has_left)
        def _():
            halo_copy(t, side, k).start()

    def wait_halo(t, side, k):
        @pl.when(has_left if side == 0 else has_right)
        def _():
            halo_copy(t, side, k).wait_recv()

    @pl.loop(0, CHUNKS)
    def _(k):
        send_halo(0, 0, k)
        send_halo(0, 1, k)

    loads[2].wait()

    def params_copy(p):
        return pltpu.make_async_remote_copy(
            src_ref=own_params,
            dst_ref=all_params.at[ens],
            send_sem=ens_send.at[0, p],
            recv_sem=ens_recv.at[0, p],
            device_id=(lax.rem(ens + p, 4), slab),
            device_id_type=MESH,
        )

    def values_copy(p):
        target = lax.rem(ens + p, 4)
        return pltpu.make_async_remote_copy(
            src_ref=values_ref.at[:, pl.ds(pl.multiple_of(target * (quarter * LANES), LANES), quarter * LANES)],
            dst_ref=all_values.at[ens],
            send_sem=ens_send.at[1, p],
            recv_sem=ens_recv.at[1, p],
            device_id=(target, slab),
            device_id_type=MESH,
        )

    def picked_copy(p):
        target = lax.rem(ens + p, 4)
        return pltpu.make_async_remote_copy(
            src_ref=picked.at[target],
            dst_ref=all_picked.at[ens],
            send_sem=ens_send.at[2, p],
            recv_sem=ens_recv.at[2, p],
            device_id=(target, slab),
            device_id_type=MESH,
        )

    for p in range(1, 4):
        params_copy(p).start()
        values_copy(p).start()

    from_lane = lax.broadcasted_iota(jnp.int32, (3 * LANES, LANES), 0)
    to_lane = lax.broadcasted_iota(jnp.int32, (3 * LANES, LANES), 1)
    same_block = ((from_lane >> 3) & (BLOCKS - 1)) == (to_lane >> 3)
    for r in range(8):
        spread_out[:, pl.ds(r * LANES, LANES)] = jnp.where(
            same_block & ((from_lane & 7) == r), 1.0, 0.0
        ).astype(jnp.bfloat16)
    for i in range(quarter):
        pick_out[i] = jnp.where(
            ((from_lane & 7) == (to_lane & 7)) & ((to_lane >> 3) == i), 1.0, 0.0
        ).astype(jnp.bfloat16)

    @pl.loop(2, rows - 2)
    def _(row):
        take_row(row)

    for h in range(halves):
        block = [own_params[:, pl.ds((b * halves + h) * LANES, LANES)] for b in range(BLOCKS)]
        params_t[pl.ds(h * LANES, LANES), :] = jnp.transpose(jnp.concatenate(block, axis=0))

    loads[1].wait()

    def expand(c, eight, h, scale):
        block = [coef_v[(c * 2 + eight) * tiles + b * halves + h] for b in range(BLOCKS)]
        turned = jnp.transpose(jnp.concatenate(block, axis=0))
        wide = jnp.dot(parts_of(turned), spread_out[...], preferred_element_type=F32)
        window = pl.ds(pl.multiple_of(h * LANES, LANES), LANES)
        for r in range(8):
            value = wide[:, r * LANES : (r + 1) * LANES]
            if scale:
                value = value * params_t[window, :]
            coef_x[c, eight * 8 + r, window, :] = value

    @pl.loop(0, 3 * 2 * halves)
    def _(n):
        expand(n // (2 * halves), lax.rem(n // halves, 2), lax.rem(n, halves), False)

    @pl.loop(0, 2 * halves)
    def _(n):
        expand(3, n // halves, lax.rem(n, halves), True)

    def wrap_row(t, r):
        cells[t, r, pl.ds(0, 8), :] = pltpu.roll(cells[t, r, pl.ds(EDGE + segment - 8, 8), :], 8, 1)
        cells[t, r, pl.ds(EDGE + segment, 8), :] = pltpu.roll(cells[t, r, pl.ds(EDGE, 8), :], LANES - 8, 1)

    def along_columns(t, rows_here, k):
        start = k * per_chunk
        for s, r in enumerate(rows_here):
            for i in range(groups + 1):
                at = start + (EDGE - 1 + i * 8)
                before, here, after = [cells[t, r, pl.ds(at + d, 8), :] for d in (-1, 0, 1)]
                slopes[s, pl.ds(i * 8, 8), :] = half_minmod(here - before, after - here)
        for s, r in enumerate(rows_here):
            for i in range(groups):
                at = start + (EDGE + i * 8)
                window = pl.ds(pl.multiple_of(start + i * 8, 8), 8)
                before, here, after = [cells[t, r, pl.ds(at + d, 8), :] for d in (-1, 0, 1)]
                half_before, half, half_after = [slopes[s, pl.ds(i * 8 + d, 8), :] for d in (0, 1, 2)]
                forward = (here + half) - (before + half_before)
                backward = (after - half_after) - (here - half)
                speed = coef_x[1, r, window, :]
                partial_c[r, window, :] = (
                    here
                    - speed * jnp.where(speed > 0.0, forward, backward)
                    + coef_x[2, r, window, :] * ((after - here) - (here - before))
                    + coef_x[3, r, window, :]
                )

    def finish_rows(t, first, last, i, before, after, store):
        window = pl.ds(pl.multiple_of(i * 8, 8), 8)
        inner = pl.ds(pl.multiple_of(EDGE + i * 8, 8), 8)
        taken = (
            [halo[t, 0, r, window, :] for r in range(before)]
            + [cells[t, r, inner, :] for r in range(max(first - 2, 0), min(last + 2, rows))]
            + [halo[t, 1, r, window, :] for r in range(after)]
        )
        new = across_rows(
            taken,
            [coef_x[0, r, window, :] for r in range(first, last)],
            [coef_x[2, r, window, :] for r in range(first, last)],
            [partial_c[r, window, :] for r in range(first, last)],
        )
        for r, value in zip(range(first, last), new):
            store(r, i, value)

    def one_step(t, final):
        def store(r, i, value):
            if final:
                final_c[pl.ds(pl.multiple_of(r * segment + i * 8, 8), 8), :] = value
            else:
                cells[t + 1, r, pl.ds(pl.multiple_of(EDGE + i * 8, 8), 8), :] = value

        for r in range(rows):
            wrap_row(t, r)

        @pl.loop(0, CHUNKS)
        def _(k):
            along_columns(t, (0, 1), k)
            along_columns(t, (rows - 2, rows - 1), k)

        @pl.loop(0, CHUNKS)
        def _(k):
            wait_halo(t, 0, k)

            @pl.loop(0, groups, step=2)
            def _(i):
                for u in range(2):
                    finish_rows(t, 0, 2, k * groups + i + u, 2, 0, store)

            if not final:
                send_halo(t + 1, 1, k)
            wait_halo(t, 1, k)

            @pl.loop(0, groups, step=2)
            def _(i):
                for u in range(2):
                    finish_rows(t, rows - 2, rows, k * groups + i + u, 0, 2, store)

            if not final:
                send_halo(t + 1, 0, k)

            @pl.loop(2, rows - 2, step=2)
            def _(r):
                along_columns(t, (r, r + 1), k)

            @pl.loop(0, groups)
            def _(i):
                finish_rows(t, 2, rows - 2, k * groups + i, 0, 0, store)

    @pl.loop(0, STEPS - 1)
    def _(t):
        one_step(t, False)

    members = 32
    group_row = jnp.zeros((8, LANES), jnp.int32) - 1
    for m in range(members):
        group_row = jnp.where(lane == m, group_ref[m], group_row)
    slot_row = jnp.zeros((8, LANES), jnp.int32)
    for m in range(members):
        slot_row = slot_row + jnp.where((group_row == group_ref[m]) & (lane > m), 1, 0)
    group_own = jnp.zeros((8, LANES), jnp.int32)
    for i in range(8):
        group_own = jnp.where(sub == i, group_ref[ens * 8 + i], group_own)
    slot_own = jnp.zeros((8, LANES), jnp.int32)
    for m in range(members):
        slot_own = slot_own + jnp.where((group_own == group_ref[m]) & (sub + ens * 8 > m), 1, 0)
    in_slot = [jnp.where(slot_row == s, 1.0, 0.0) for s in range(4)]
    by_group = jnp.concatenate(
        [jnp.where(group_row == sub, in_slot[s], 0.0) for s in range(4)], axis=0
    )[:, :members]
    by_own = jnp.concatenate(
        [jnp.where(group_row == group_own, in_slot[s], 0.0) for s in range(4)], axis=0
    )[:, :members]

    def pick(chosen, held):
        return jnp.dot(chosen, held, precision=lax.Precision.HIGHEST, preferred_element_type=F32)

    spread_of = 1.0 / math.sqrt(3.0)

    def centred(four):
        mean = (four[0] + four[1] + four[2] + four[3]) * 0.25
        return [(x - mean) * spread_of for x in four]

    all_params[ens] = own_params[...]
    for p in range(1, 4):
        params_copy(p).wait_recv()
    columns = tiles * LANES
    piece = min(512, columns)

    @pl.loop(0, columns // piece)
    def _(c):
        window = pl.ds(pl.multiple_of(c * piece, piece), piece)
        held = jnp.concatenate([all_params[q, :, window] for q in range(4)], axis=0)
        ordered = pick(by_own, held)
        for s, value in enumerate(centred([ordered[s * 8 : s * 8 + 8] for s in range(4)])):
            moved[s, :, window] = value

    loads[3].wait()
    loads[4].wait()
    for p in range(1, 4):
        values_copy(p).wait_recv()
    ordered_values = pick(by_group, jnp.concatenate([all_values[q] for q in range(4)], axis=0))
    total_obs = float(obs_tiles * LANES * slabs)
    weights = [
        jnp.broadcast_to(1.0 / (variance_v[pl.ds(ens * quarter + i, 1), :] * total_obs), (8, LANES))
        for i in range(quarter)
    ]
    weight = jnp.concatenate(weights, axis=1)

    loads[5].wait()
    cell = index_v[...]
    column_of = cell & (tiles * LANES - 1)
    place_v[...] = cell // (tiles * LANES) * segment + (column_of & (segment - 1))
    to_smem = pltpu.make_async_copy(place_v, place, load_sem.at[6])
    to_smem.start()
    block_of = jnp.transpose((column_of // segment).astype(F32))
    lane_block = (lax.broadcasted_iota(jnp.int32, (LANES, LANES), 1) >> 3).astype(F32)
    for i in range(obs_tiles):
        mask_v[i] = jnp.where(
            jnp.broadcast_to(block_of[:, i : i + 1], (LANES, LANES)) == lane_block, 1.0, 0.0
        )
    to_smem.wait()

    one_step(STEPS - 1, True)

    def gather_quarter(q):
        def one_tile(i, total):
            tile = q * quarter + i

            @pl.loop(0, LANES // 32)
            def _(g):
                for v in range(4):
                    taken = jnp.zeros((8, LANES), F32)
                    for u in range(8):
                        row = final_c[pl.ds(place[tile, g * 32 + v * 8 + u], 1), :]
                        taken = jnp.where(sub == u, jnp.broadcast_to(row, (8, LANES)), taken)
                    window = pl.ds(pl.multiple_of(g * 32 + v * 8, 8), 8)
                    found[window, :] = taken * mask_v[tile, window, :]

            return total + jnp.dot(parts_of(found[...]), pick_out[i], preferred_element_type=F32)

        total = lax.fori_loop(0, quarter, one_tile, jnp.zeros((LANES, LANES), F32))
        turned = jnp.transpose(total)
        for i in range(quarter):
            picked[q, i] = turned[i * 8 : i * 8 + 8]

    def emit_rows(first, last):
        @pl.loop(first, last)
        def _(r):
            for h in range(halves):
                start = pl.multiple_of(r * segment + h * LANES, LANES)
                turned = jnp.transpose(final_c[pl.ds(start, LANES), :])
                for b in range(BLOCKS):
                    field_v[pl.ds(of_tile(r, b * halves + h), 8, stride=rows * tiles), :] = turned[
                        b * 8 : b * 8 + 8
                    ]

    for p in range(1, 4):
        gather_quarter(lax.rem(ens + p, 4))
        picked_copy(p).start()
    gather_quarter(ens)
    for i in range(quarter):
        all_picked[ens, i] = picked[ens, i]
    emit_rows(0, 6)
    for p in range(1, 4):
        picked_copy(p).wait_recv()

    held = jnp.concatenate(
        [
            jnp.concatenate([all_picked[q, i] for i in range(quarter)], axis=1)
            for q in range(4)
        ],
        axis=0,
    )
    ordered = pick(by_group, held)
    ordered = [ordered[s * 8 : s * 8 + 8] for s in range(4)]
    innovation = [
        (ordered_values[s * 8 : s * 8 + 8] - ordered[s]) * weight for s in range(4)
    ]
    anomalies = centred(ordered)
    weighted = [a * weight for a in anomalies]
    products = [(weighted[a], anomalies[b]) for a, b in PAIRS] + [
        (anomalies[a], innovation[b]) for a in range(4) for b in range(4)
    ]
    packed = jnp.zeros((8, LANES), F32)
    for position, (left, right) in enumerate(products):
        both = left * right
        folded = both[:, :LANES]
        for i in range(1, quarter):
            folded = folded + both[:, i * LANES : (i + 1) * LANES]
        packed = jnp.where(lane == position, jnp.sum(folded, axis=1, keepdims=True), packed)

    def sum_over(value, part, sums, me, count, device, send, recv, meanwhile):
        part[...] = value

        def copy(i, slot):
            return pltpu.make_async_remote_copy(
                src_ref=part,
                dst_ref=sums.at[me],
                send_sem=send.at[slot],
                recv_sem=recv.at[slot],
                device_id=device(i),
                device_id_type=MESH,
            )

        @pl.loop(1, count)
        def _(p):
            copy(lax.rem(me + p, count), p).start()

        sums[me] = value
        meanwhile()

        @pl.loop(1, count)
        def _(p):
            copy(lax.rem(me + p, count), p).wait()

        total = sums[0]
        for i in range(1, count):
            total = total + sums[i]
        return total

    field_store = pltpu.make_async_copy(field_v, field_out, out_sem)

    def rest_of_field():
        emit_rows(11, rows)
        field_store.start()

    total = sum_over(
        packed,
        part_near,
        sums_near,
        near_me,
        near_count,
        near_device,
        near_send,
        near_recv,
        lambda: emit_rows(6, 11),
    )
    total = sum_over(
        total, part_far, sums_far, far_me, far_count, far_device, far_send, far_recv, rest_of_field
    )

    mine = jnp.zeros((8, LANES), F32)
    for g in range(GROUPS):
        mine = jnp.where(group_own == g, jnp.broadcast_to(total[g : g + 1], (8, LANES)), mine)

    def column(i):
        return jnp.broadcast_to(mine[:, i : i + 1], (8, LANES))

    a = {}
    for i, (p, q) in enumerate(PAIRS):
        a[p, q] = column(i) + (1.0 if p == q else 0.0)
    b = []
    for p in range(4):
        value = column(len(PAIRS) + p * 4)
        for q in range(1, 4):
            value = jnp.where(slot_own == q, column(len(PAIRS) + p * 4 + q), value)
        b.append(value)
    low = {}
    for p in range(4):
        for q in range(p + 1, 4):
            low[q, p] = a[p, q] / a[p, p]
        for q in range(p + 1, 4):
            for r in range(q, 4):
                a[q, r] = a[q, r] - low[q, p] * a[p, r]
    for p in range(4):
        for q in range(p + 1, 4):
            b[q] = b[q] - low[q, p] * b[p]
    solved = [b[p] / a[p, p] for p in range(4)]
    for p in range(2, -1, -1):
        for q in range(p + 1, 4):
            solved[p] = solved[p] - low[q, p] * solved[q]

    for j in range(tiles):
        window = pl.ds(j * LANES, LANES)
        value = own_params[:, window]
        for s in range(4):
            value = value + solved[s] * moved[s, :, window]
        params_out[:, window] = value

    for p in range(1, 4):
        params_copy(p).wait_send()
        values_copy(p).wait_send()
        picked_copy(p).wait_send()

    @pl.loop(0, STEPS)
    def _(t):
        @pl.loop(0, CHUNKS)
        def _(k):
            @pl.when(has_right)
            def _():
                halo_copy(t, 0, k).wait_send()

            @pl.when(has_left)
            def _():
                halo_copy(t, 1, k).wait_send()

    field_store.wait()


def local(tracer, coefficients, parameters, obs_index, obs_values, obs_variance, member_group):
    members, rows, columns = tracer.shape
    slabs = lax.axis_size("slab")
    tiles = columns // LANES
    obs_tiles = obs_index.shape[0] // LANES
    far_count = slabs // NEAR
    near_count = 4 * NEAR
    segment = columns // BLOCKS
    wide = (rows, segment, LANES)
    smem = pl.BlockSpec(memory_space=pltpu.SMEM)
    anywhere = pl.BlockSpec(memory_space=pl.ANY)
    vmem = pl.BlockSpec(memory_space=pltpu.VMEM)
    field, params = pl.pallas_call(
        functools.partial(kernel, slabs, tiles),
        out_shape=(
            jax.ShapeDtypeStruct((members * rows * tiles, LANES), F32),
            jax.ShapeDtypeStruct((members, columns), F32),
        ),
        in_specs=[smem, anywhere, anywhere, anywhere, anywhere, anywhere, anywhere],
        out_specs=(anywhere, vmem),
        scratch_shapes=[
            pltpu.VMEM((members * rows * tiles, LANES), F32),
            pltpu.VMEM((4 * rows // 8 * tiles, 8, LANES), F32),
            pltpu.VMEM((members, columns), F32),
            pltpu.VMEM((obs_tiles, LANES), F32),
            pltpu.VMEM((obs_tiles, LANES), jnp.int32),
            pltpu.VMEM((obs_tiles, LANES), jnp.int32),
            pltpu.SMEM((obs_tiles, LANES), jnp.int32),
            pltpu.VMEM((3 * LANES, 8 * LANES), jnp.bfloat16),
            pltpu.VMEM((obs_tiles // 4, 3 * LANES, LANES), jnp.bfloat16),
            pltpu.VMEM((segment, LANES), F32),
            pltpu.VMEM((4,) + wide, F32),
            pltpu.VMEM((STEPS, rows, segment + 2 * EDGE, LANES), F32),
            pltpu.VMEM((STEPS, 2, 2, segment, LANES), F32),
            pltpu.VMEM((2, segment // CHUNKS + 8, LANES), F32),
            pltpu.VMEM(wide, F32),
            pltpu.VMEM((rows * segment, LANES), F32),
            pltpu.VMEM((obs_tiles, LANES, LANES), F32),
            pltpu.VMEM((LANES, LANES), F32),
            pltpu.VMEM((members * rows * tiles, LANES), F32),
            pltpu.VMEM((4, members, columns), F32),
            pltpu.VMEM((4, members, obs_tiles // 4 * LANES), F32),
            pltpu.VMEM((4, obs_tiles // 4, 8, LANES), F32),
            pltpu.VMEM((4, obs_tiles // 4, 8, LANES), F32),
            pltpu.VMEM((4, members, columns), F32),
            pltpu.VMEM((8, LANES), F32),
            pltpu.VMEM((8, LANES), F32),
            pltpu.VMEM((near_count, 8, LANES), F32),
            pltpu.VMEM((far_count, 8, LANES), F32),
            pltpu.SemaphoreType.DMA((7,)),
            pltpu.SemaphoreType.DMA,
            pltpu.SemaphoreType.DMA((STEPS, 2, CHUNKS)),
            pltpu.SemaphoreType.DMA((STEPS, 2, CHUNKS)),
            pltpu.SemaphoreType.DMA((3, 4)),
            pltpu.SemaphoreType.DMA((3, 4)),
            pltpu.SemaphoreType.DMA((near_count,)),
            pltpu.SemaphoreType.DMA((near_count,)),
            pltpu.SemaphoreType.DMA((far_count,)),
            pltpu.SemaphoreType.DMA((far_count,)),
        ],
        compiler_params=pltpu.CompilerParams(
            collective_id=0, has_side_effects=True, vmem_limit_bytes=56 * 1024 * 1024
        ),
    )(
        member_group,
        obs_index.reshape(obs_tiles, LANES),
        tracer.reshape(members, rows // 8, 8, tiles, LANES).transpose(0, 1, 3, 2, 4).reshape(-1, LANES),
        coefficients.reshape(4, rows // 8, 8, tiles, LANES).transpose(0, 1, 3, 2, 4).reshape(-1, 8, LANES),
        parameters,
        obs_values,
        obs_variance.reshape(obs_tiles, LANES),
    )
    field = field.reshape(members, rows // 8, tiles, 8, LANES).transpose(0, 1, 3, 2, 4)
    return field.reshape(members, rows, columns), params


def solution(mesh):
    in_specs = (
        P("ens", "slab", None),
        P(None, "slab", None),
        P("ens", None),
        P("slab"),
        P("ens", "slab"),
        P("slab"),
        P(),
    )
    out_specs = (P("ens", "slab", None), P("ens", None))
    return jax.shard_map(local, mesh=mesh, in_specs=in_specs, out_specs=out_specs, check_vma=False)
```

```python
import functools
import math

import jax
import jax.numpy as jnp
from jax import lax
from jax.experimental import pallas as pl
from jax.experimental.pallas import tpu as pltpu
from jax.sharding import PartitionSpec as P

STEPS = 4
GROUPS = 8
LANES = 128
CHUNKS = 2
NEAR = 4
BLOCKS = 16
EDGE = 8
MESH = pl.DeviceIdType.MESH
F32 = jnp.float32
PAIRS = [(a, b) for a in range(4) for b in range(a, 4)]


def lanes_of():
    return lax.broadcasted_iota(jnp.int32, (8, LANES), 1)


def sublanes_of():
    return lax.broadcasted_iota(jnp.int32, (8, LANES), 0)


def parts_of(value):
    high = value.astype(jnp.bfloat16)
    rest = value - high.astype(F32)
    middle = rest.astype(jnp.bfloat16)
    low = (rest - middle.astype(F32)).astype(jnp.bfloat16)
    return jnp.concatenate([high, middle, low], axis=1)


def half_minmod(left, right):
    return 0.5 * jnp.maximum(jnp.minimum(left, right), jnp.minimum(jnp.maximum(left, right), 0.0))


def across_rows(rows, speeds, spreads, bases):
    count = len(rows) - 4
    diffs = [rows[i + 1] - rows[i] for i in range(count + 3)]
    halves = [half_minmod(diffs[i], diffs[i + 1]) for i in range(count + 2)]
    bends = [halves[i + 1] - halves[i] for i in range(count + 1)]
    out = []
    for i in range(count):
        speed = speeds[i]
        change = jnp.where(speed > 0.0, diffs[i + 1] + bends[i], diffs[i + 2] - bends[i + 1])
        out.append(bases[i] - speed * change + spreads[i] * (diffs[i + 2] - diffs[i + 1]))
    return out


def kernel(
    slabs,
    tiles,
    group_ref,
    index_ref,
    tracer_ref,
    coef_ref,
    params_ref,
    values_ref,
    variance_ref,
    field_out,
    params_out,
    tracer_v,
    coef_v,
    own_params,
    variance_v,
    index_v,
    place_v,
    place,
    spread_out,
    pick_out,
    params_t,
    coef_x,
    cells,
    halo,
    slopes,
    partial_c,
    final_c,
    mask_v,
    found,
    field_v,
    all_params,
    all_values,
    picked,
    all_picked,
    moved,
    part_near,
    part_far,
    sums_near,
    sums_far,
    load_sem,
    out_sem,
    halo_send,
    halo_recv,
    ens_send,
    ens_recv,
    near_send,
    near_recv,
    far_send,
    far_recv,
):
    ens = lax.axis_index("ens")
    slab = lax.axis_index("slab")
    rows = 16
    segment = tiles * LANES // BLOCKS
    halves = segment // LANES
    per_chunk = segment // CHUNKS
    groups = per_chunk // 8
    far_count = slabs // NEAR
    near_count = 4 * NEAR
    quarter = picked.shape[1]
    obs_tiles = 4 * quarter
    has_left = slab > 0
    has_right = slab < slabs - 1
    near_me = ens * NEAR + lax.rem(slab, NEAR)
    far_me = slab // NEAR
    lane = lanes_of()
    sub = sublanes_of()

    def near_device(i):
        return (i // NEAR, far_me * NEAR + lax.rem(i, NEAR))

    def far_device(i):
        return (ens, i * NEAR + lax.rem(slab, NEAR))

    loads = [
        pltpu.make_async_copy(tracer_ref, tracer_v, load_sem.at[0]),
        pltpu.make_async_copy(coef_ref, coef_v, load_sem.at[1]),
        pltpu.make_async_copy(params_ref, own_params, load_sem.at[2]),
        pltpu.make_async_copy(variance_ref, variance_v, load_sem.at[3]),
        pltpu.make_async_copy(
            values_ref.at[:, pl.ds(pl.multiple_of(ens * (quarter * LANES), LANES), quarter * LANES)],
            all_values.at[ens],
            load_sem.at[4],
        ),
        pltpu.make_async_copy(index_ref, index_v, load_sem.at[5]),
    ]
    for load in loads:
        load.start()

    barrier = pltpu.get_barrier_semaphore()

    @pl.loop(1, near_count)
    def _(p):
        pl.semaphore_signal(
            barrier, inc=1, device_id=near_device(lax.rem(near_me + p, near_count)), device_id_type=MESH
        )

    @pl.loop(1, far_count)
    def _(p):
        pl.semaphore_signal(
            barrier, inc=1, device_id=far_device(lax.rem(far_me + p, far_count)), device_id_type=MESH
        )

    @pl.when(has_left)
    def _():
        pl.semaphore_signal(barrier, inc=1, device_id=(ens, slab - 1), device_id_type=MESH)

    @pl.when(has_right)
    def _():
        pl.semaphore_signal(barrier, inc=1, device_id=(ens, slab + 1), device_id_type=MESH)

    loads[0].wait()

    def of_tile(row, j):
        return (row // 8 * tiles + j) * 8 + lax.rem(row, 8)

    def take_row(row):
        for h in range(halves):
            block = [
                tracer_v[pl.ds(of_tile(row, b * halves + h), 8, stride=rows * tiles), :]
                for b in range(BLOCKS)
            ]
            cells[0, row, pl.ds(EDGE + h * LANES, LANES), :] = jnp.transpose(jnp.concatenate(block, axis=0))

    def edge_row(i):
        return i + i // 2 * (rows - 4)

    @pl.loop(0, 4)
    def _(i):
        take_row(edge_row(i))

    zero = jnp.zeros((8, LANES), F32)

    def clear(side):
        @pl.loop(0, STEPS)
        def _(t):
            for r in range(2):
                for i in range(segment // 8):
                    halo[t, side, r, pl.ds(i * 8, 8), :] = zero

    pl.when(jnp.logical_not(has_left))(functools.partial(clear, 0))
    pl.when(jnp.logical_not(has_right))(functools.partial(clear, 1))

    neighbours = jnp.where(has_left, 1, 0) + jnp.where(has_right, 1, 0)
    pl.semaphore_wait(barrier, near_count + far_count - 2 + neighbours)

    def halo_copy(t, side, k):
        start = pl.multiple_of(k * per_chunk, per_chunk)
        return pltpu.make_async_remote_copy(
            src_ref=cells.at[
                t,
                pl.ds(rows - 2, 2) if side == 0 else pl.ds(0, 2),
                pl.ds(pl.multiple_of(EDGE + start, 8), per_chunk),
            ],
            dst_ref=halo.at[t, side, :, pl.ds(start, per_chunk)],
            send_sem=halo_send.at[t, side, k],
            recv_sem=halo_recv.at[t, side, k],
            device_id=(ens, slab + 1 if side == 0 else slab - 1),
            device_id_type=MESH,
        )

    def send_halo(t, side, k):
        @pl.when(has_right if side == 0 else has_left)
        def _():
            halo_copy(t, side, k).start()

    def wait_halo(t, side, k):
        @pl.when(has_left if side == 0 else has_right)
        def _():
            halo_copy(t, side, k).wait_recv()

    @pl.loop(0, CHUNKS)
    def _(k):
        send_halo(0, 0, k)
        send_halo(0, 1, k)

    loads[2].wait()

    def params_copy(p):
        return pltpu.make_async_remote_copy(
            src_ref=own_params,
            dst_ref=all_params.at[ens],
            send_sem=ens_send.at[0, p],
            recv_sem=ens_recv.at[0, p],
            device_id=(lax.rem(ens + p, 4), slab),
            device_id_type=MESH,
        )

    def values_copy(p):
        target = lax.rem(ens + p, 4)
        return pltpu.make_async_remote_copy(
            src_ref=values_ref.at[:, pl.ds(pl.multiple_of(target * (quarter * LANES), LANES), quarter * LANES)],
            dst_ref=all_values.at[ens],
            send_sem=ens_send.at[1, p],
            recv_sem=ens_recv.at[1, p],
            device_id=(target, slab),
            device_id_type=MESH,
        )

    def picked_copy(p):
        target = lax.rem(ens + p, 4)
        return pltpu.make_async_remote_copy(
            src_ref=picked.at[target],
            dst_ref=all_picked.at[ens],
            send_sem=ens_send.at[2, p],
            recv_sem=ens_recv.at[2, p],
            device_id=(target, slab),
            device_id_type=MESH,
        )

    for p in range(1, 4):
        params_copy(p).start()
        values_copy(p).start()

    from_lane = lax.broadcasted_iota(jnp.int32, (3 * LANES, LANES), 0)
    to_lane = lax.broadcasted_iota(jnp.int32, (3 * LANES, LANES), 1)
    same_block = ((from_lane >> 3) & (BLOCKS - 1)) == (to_lane >> 3)
    for r in range(8):
        spread_out[:, pl.ds(r * LANES, LANES)] = jnp.where(
            same_block & ((from_lane & 7) == r), 1.0, 0.0
        ).astype(jnp.bfloat16)
    for i in range(quarter):
        pick_out[pl.ds(i * 3 * LANES, 3 * LANES), :] = jnp.where(
            ((from_lane & 7) == (to_lane & 7)) & ((to_lane >> 3) == i), 1.0, 0.0
        ).astype(jnp.bfloat16)

    @pl.loop(2, rows - 2)
    def _(row):
        take_row(row)

    for h in range(halves):
        block = [own_params[:, pl.ds((b * halves + h) * LANES, LANES)] for b in range(BLOCKS)]
        params_t[pl.ds(h * LANES, LANES), :] = jnp.transpose(jnp.concatenate(block, axis=0))

    loads[1].wait()

    def expand(c, eight, h, scale):
        block = [coef_v[(c * 2 + eight) * tiles + b * halves + h] for b in range(BLOCKS)]
        turned = jnp.transpose(jnp.concatenate(block, axis=0))
        wide = jnp.dot(parts_of(turned), spread_out[...], preferred_element_type=F32)
        window = pl.ds(pl.multiple_of(h * LANES, LANES), LANES)
        for r in range(8):
            value = wide[:, r * LANES : (r + 1) * LANES]
            if scale:
                value = value * params_t[window, :]
            coef_x[c, eight * 8 + r, window, :] = value

    @pl.loop(0, 3 * 2 * halves)
    def _(n):
        expand(n // (2 * halves), lax.rem(n // halves, 2), lax.rem(n, halves), False)

    @pl.loop(0, 2 * halves)
    def _(n):
        expand(3, n // halves, lax.rem(n, halves), True)

    def wrap_row(t, r):
        cells[t, r, pl.ds(0, 8), :] = pltpu.roll(cells[t, r, pl.ds(EDGE + segment - 8, 8), :], 8, 1)
        cells[t, r, pl.ds(EDGE + segment, 8), :] = pltpu.roll(cells[t, r, pl.ds(EDGE, 8), :], LANES - 8, 1)

    def along_columns(t, rows_here, k):
        start = k * per_chunk
        for s, r in enumerate(rows_here):
            for i in range(groups + 1):
                at = start + (EDGE - 1 + i * 8)
                before, here, after = [cells[t, r, pl.ds(at + d, 8), :] for d in (-1, 0, 1)]
                slopes[s, pl.ds(i * 8, 8), :] = half_minmod(here - before, after - here)
        for s, r in enumerate(rows_here):
            for i in range(groups):
                at = start + (EDGE + i * 8)
                window = pl.ds(pl.multiple_of(start + i * 8, 8), 8)
                before, here, after = [cells[t, r, pl.ds(at + d, 8), :] for d in (-1, 0, 1)]
                half_before, half, half_after = [slopes[s, pl.ds(i * 8 + d, 8), :] for d in (0, 1, 2)]
                down, up = here - before, after - here
                forward = down + (half - half_before)
                backward = up - (half_after - half)
                speed = coef_x[1, r, window, :]
                partial_c[r, window, :] = (
                    here
                    - speed * jnp.where(speed > 0.0, forward, backward)
                    + coef_x[2, r, window, :] * (up - down)
                    + coef_x[3, r, window, :]
                )

    def finish_rows(t, first, last, i, before, after, store):
        window = pl.ds(pl.multiple_of(i * 8, 8), 8)
        inner = pl.ds(pl.multiple_of(EDGE + i * 8, 8), 8)
        taken = (
            [halo[t, 0, r, window, :] for r in range(before)]
            + [cells[t, r, inner, :] for r in range(max(first - 2, 0), min(last + 2, rows))]
            + [halo[t, 1, r, window, :] for r in range(after)]
        )
        new = across_rows(
            taken,
            [coef_x[0, r, window, :] for r in range(first, last)],
            [coef_x[2, r, window, :] for r in range(first, last)],
            [partial_c[r, window, :] for r in range(first, last)],
        )
        for r, value in zip(range(first, last), new):
            store(r, i, value)

    def one_step(t, final):
        def store(r, i, value):
            if final:
                final_c[pl.ds(pl.multiple_of(r * segment + i * 8, 8), 8), :] = value
            else:
                cells[t + 1, r, pl.ds(pl.multiple_of(EDGE + i * 8, 8), 8), :] = value

        for r in range(rows):
            wrap_row(t, r)

        def edges(k):
            along_columns(t, (0, 1), k)
            along_columns(t, (rows - 2, rows - 1), k)
            for side in range(2):
                wait_halo(t, side, k)
                first = (rows - 2) * side

                @pl.loop(0, groups, step=4)
                def _(i):
                    for u in range(4):
                        finish_rows(
                            t, first, first + 2, k * groups + i + u, 2 - 2 * side, 2 * side, store
                        )

                if not final:
                    send_halo(t + 1, 1 - side, k)

        def inside(k):
            @pl.loop(2, rows - 2, step=2)
            def _(r):
                along_columns(t, (r, r + 1), k)

            @pl.loop(0, groups)
            def _(i):
                finish_rows(t, 2, rows - 2, k * groups + i, 0, 0, store)

        @pl.loop(0, CHUNKS)
        def _(k):
            pl.when(k == CHUNKS - 1)(lambda: inside(k))
            edges(k)
            pl.when(k < CHUNKS - 1)(lambda: inside(k))

    @pl.loop(0, STEPS - 1)
    def _(t):
        one_step(t, False)

    members = 32
    group_row = jnp.zeros((8, LANES), jnp.int32) - 1
    for m in range(members):
        group_row = jnp.where(lane == m, group_ref[m], group_row)
    slot_row = jnp.zeros((8, LANES), jnp.int32)
    for m in range(members):
        slot_row = slot_row + jnp.where((group_row == group_ref[m]) & (lane > m), 1, 0)
    group_own = jnp.zeros((8, LANES), jnp.int32)
    for i in range(8):
        group_own = jnp.where(sub == i, group_ref[ens * 8 + i], group_own)
    slot_own = jnp.zeros((8, LANES), jnp.int32)
    for m in range(members):
        slot_own = slot_own + jnp.where((group_own == group_ref[m]) & (sub + ens * 8 > m), 1, 0)
    in_slot = [jnp.where(slot_row == s, 1.0, 0.0) for s in range(4)]
    by_group = jnp.concatenate(
        [jnp.where(group_row == sub, in_slot[s], 0.0) for s in range(4)], axis=0
    )[:, :members]
    by_own = jnp.concatenate(
        [jnp.where(group_row == group_own, in_slot[s], 0.0) for s in range(4)], axis=0
    )[:, :members]

    def pick(chosen, held):
        return jnp.dot(chosen, held, precision=lax.Precision.HIGHEST, preferred_element_type=F32)

    spread_of = 1.0 / math.sqrt(3.0)

    def centred(four):
        mean = (four[0] + four[1] + four[2] + four[3]) * 0.25
        return [(x - mean) * spread_of for x in four]

    all_params[ens] = own_params[...]
    for p in range(1, 4):
        params_copy(p).wait_recv()
    columns = tiles * LANES
    piece = min(512, columns)

    @pl.loop(0, columns // piece)
    def _(c):
        window = pl.ds(pl.multiple_of(c * piece, piece), piece)
        held = jnp.concatenate([all_params[q, :, window] for q in range(4)], axis=0)
        ordered = pick(by_own, held)
        for s, value in enumerate(centred([ordered[s * 8 : s * 8 + 8] for s in range(4)])):
            moved[s, :, window] = value

    loads[3].wait()
    loads[4].wait()
    for p in range(1, 4):
        values_copy(p).wait_recv()
    ordered_values = pick(by_group, jnp.concatenate([all_values[q] for q in range(4)], axis=0))
    total_obs = float(obs_tiles * LANES * slabs)
    weights = [
        jnp.broadcast_to(1.0 / (variance_v[pl.ds(ens * quarter + i, 1), :] * total_obs), (8, LANES))
        for i in range(quarter)
    ]
    weight = jnp.concatenate(weights, axis=1)

    loads[5].wait()
    cell = index_v[...]
    column_of = cell & (tiles * LANES - 1)
    place_v[...] = cell // (tiles * LANES) * segment + (column_of & (segment - 1))
    to_smem = pltpu.make_async_copy(place_v, place, load_sem.at[6])
    to_smem.start()
    block_of = jnp.transpose((column_of // segment).astype(F32))
    lane_block = (lax.broadcasted_iota(jnp.int32, (LANES, LANES), 1) >> 3).astype(F32)
    for i in range(obs_tiles):
        mask_v[i] = jnp.where(
            jnp.broadcast_to(block_of[:, i : i + 1], (LANES, LANES)) == lane_block, 1.0, 0.0
        )
    to_smem.wait()

    one_step(STEPS - 1, True)

    def gather_quarter(q):
        @pl.loop(0, quarter)
        def _(i):
            tile = q * quarter + i
            for g in range(LANES // 8):
                taken = jnp.zeros((8, LANES), F32)
                for u in range(8):
                    row = final_c[pl.ds(place[tile, g * 8 + u], 1), :]
                    taken = jnp.where(sub == u, jnp.broadcast_to(row, (8, LANES)), taken)
                window = pl.ds(pl.multiple_of(i * LANES + g * 8, 8), 8)
                found[window, :] = taken * mask_v[tile, pl.ds(g * 8, 8), :]

        parts = [parts_of(found[pl.ds(i * LANES, LANES), :]) for i in range(quarter)]
        total = jnp.dot(jnp.concatenate(parts, axis=1), pick_out[...], preferred_element_type=F32)
        turned = jnp.transpose(total)
        for i in range(quarter):
            picked[q, i] = turned[i * 8 : i * 8 + 8]

    def emit_rows(first, last):
        @pl.loop(first, last)
        def _(r):
            for h in range(halves):
                start = pl.multiple_of(r * segment + h * LANES, LANES)
                turned = jnp.transpose(final_c[pl.ds(start, LANES), :])
                for b in range(BLOCKS):
                    field_v[pl.ds(of_tile(r, b * halves + h), 8, stride=rows * tiles), :] = turned[
                        b * 8 : b * 8 + 8
                    ]

    @pl.loop(1, 5)
    def _(p):
        gather_quarter(lax.rem(ens + p, 4))
        pl.when(p < 4)(lambda: picked_copy(p).start())

    for i in range(quarter):
        all_picked[ens, i] = picked[ens, i]
    emit_rows(0, 6)
    for p in range(1, 4):
        picked_copy(p).wait_recv()

    held = jnp.concatenate(
        [
            jnp.concatenate([all_picked[q, i] for i in range(quarter)], axis=1)
            for q in range(4)
        ],
        axis=0,
    )
    ordered = pick(by_group, held)
    ordered = [ordered[s * 8 : s * 8 + 8] for s in range(4)]
    innovation = [
        (ordered_values[s * 8 : s * 8 + 8] - ordered[s]) * weight for s in range(4)
    ]
    anomalies = centred(ordered)
    weighted = [a * weight for a in anomalies]
    products = [(weighted[a], anomalies[b]) for a, b in PAIRS] + [
        (anomalies[a], innovation[b]) for a in range(4) for b in range(4)
    ]
    packed = jnp.zeros((8, LANES), F32)
    for position, (left, right) in enumerate(products):
        both = left * right
        folded = both[:, :LANES]
        for i in range(1, quarter):
            folded = folded + both[:, i * LANES : (i + 1) * LANES]
        packed = jnp.where(lane == position, jnp.sum(folded, axis=1, keepdims=True), packed)

    def sum_over(value, part, sums, me, count, device, send, recv, meanwhile):
        part[...] = value

        def copy(i, slot):
            return pltpu.make_async_remote_copy(
                src_ref=part,
                dst_ref=sums.at[me],
                send_sem=send.at[slot],
                recv_sem=recv.at[slot],
                device_id=device(i),
                device_id_type=MESH,
            )

        @pl.loop(1, count)
        def _(p):
            copy(lax.rem(me + p, count), p).start()

        sums[me] = value
        meanwhile()

        @pl.loop(1, count)
        def _(p):
            copy(lax.rem(me + p, count), p).wait()

        total = sums[0]
        for i in range(1, count):
            total = total + sums[i]
        return total

    field_store = pltpu.make_async_copy(field_v, field_out, out_sem)

    def rest_of_field():
        emit_rows(11, rows)
        field_store.start()

    total = sum_over(
        packed,
        part_near,
        sums_near,
        near_me,
        near_count,
        near_device,
        near_send,
        near_recv,
        lambda: emit_rows(6, 11),
    )
    total = sum_over(
        total, part_far, sums_far, far_me, far_count, far_device, far_send, far_recv, rest_of_field
    )

    mine = jnp.zeros((8, LANES), F32)
    for g in range(GROUPS):
        mine = jnp.where(group_own == g, jnp.broadcast_to(total[g : g + 1], (8, LANES)), mine)

    def column(i):
        return jnp.broadcast_to(mine[:, i : i + 1], (8, LANES))

    a = {}
    for i, (p, q) in enumerate(PAIRS):
        a[p, q] = column(i) + (1.0 if p == q else 0.0)
    b = []
    for p in range(4):
        value = column(len(PAIRS) + p * 4)
        for q in range(1, 4):
            value = jnp.where(slot_own == q, column(len(PAIRS) + p * 4 + q), value)
        b.append(value)
    low = {}
    for p in range(4):
        for q in range(p + 1, 4):
            low[q, p] = a[p, q] / a[p, p]
        for q in range(p + 1, 4):
            for r in range(q, 4):
                a[q, r] = a[q, r] - low[q, p] * a[p, r]
    for p in range(4):
        for q in range(p + 1, 4):
            b[q] = b[q] - low[q, p] * b[p]
    solved = [b[p] / a[p, p] for p in range(4)]
    for p in range(2, -1, -1):
        for q in range(p + 1, 4):
            solved[p] = solved[p] - low[q, p] * solved[q]

    for j in range(tiles):
        window = pl.ds(j * LANES, LANES)
        value = own_params[:, window]
        for s in range(4):
            value = value + solved[s] * moved[s, :, window]
        params_out[:, window] = value

    for p in range(1, 4):
        params_copy(p).wait_send()
        values_copy(p).wait_send()
        picked_copy(p).wait_send()

    @pl.loop(0, STEPS)
    def _(t):
        @pl.loop(0, CHUNKS)
        def _(k):
            @pl.when(has_right)
            def _():
                halo_copy(t, 0, k).wait_send()

            @pl.when(has_left)
            def _():
                halo_copy(t, 1, k).wait_send()

    field_store.wait()


def local(tracer, coefficients, parameters, obs_index, obs_values, obs_variance, member_group):
    members, rows, columns = tracer.shape
    slabs = lax.axis_size("slab")
    tiles = columns // LANES
    obs_tiles = obs_index.shape[0] // LANES
    far_count = slabs // NEAR
    near_count = 4 * NEAR
    segment = columns // BLOCKS
    wide = (rows, segment, LANES)
    smem = pl.BlockSpec(memory_space=pltpu.SMEM)
    anywhere = pl.BlockSpec(memory_space=pl.ANY)
    vmem = pl.BlockSpec(memory_space=pltpu.VMEM)
    field, params = pl.pallas_call(
        functools.partial(kernel, slabs, tiles),
        out_shape=(
            jax.ShapeDtypeStruct((members * rows * tiles, LANES), F32),
            jax.ShapeDtypeStruct((members, columns), F32),
        ),
        in_specs=[smem] + [pl.BlockSpec(memory_space=pltpu.HBM)] * 6,
        out_specs=(anywhere, vmem),
        scratch_shapes=[
            pltpu.VMEM((members * rows * tiles, LANES), F32),
            pltpu.VMEM((4 * rows // 8 * tiles, 8, LANES), F32),
            pltpu.VMEM((members, columns), F32),
            pltpu.VMEM((obs_tiles, LANES), F32),
            pltpu.VMEM((obs_tiles, LANES), jnp.int32),
            pltpu.VMEM((obs_tiles, LANES), jnp.int32),
            pltpu.SMEM((obs_tiles, LANES), jnp.int32),
            pltpu.VMEM((3 * LANES, 8 * LANES), jnp.bfloat16),
            pltpu.VMEM((obs_tiles // 4 * 3 * LANES, LANES), jnp.bfloat16),
            pltpu.VMEM((segment, LANES), F32),
            pltpu.VMEM((4,) + wide, F32),
            pltpu.VMEM((STEPS, rows, segment + 2 * EDGE, LANES), F32),
            pltpu.VMEM((STEPS, 2, 2, segment, LANES), F32),
            pltpu.VMEM((2, segment // CHUNKS + 8, LANES), F32),
            pltpu.VMEM(wide, F32),
            pltpu.VMEM((rows * segment, LANES), F32),
            pltpu.VMEM((obs_tiles, LANES, LANES), F32),
            pltpu.VMEM((obs_tiles // 4 * LANES, LANES), F32),
            pltpu.VMEM((members * rows * tiles, LANES), F32),
            pltpu.VMEM((4, members, columns), F32),
            pltpu.VMEM((4, members, obs_tiles // 4 * LANES), F32),
            pltpu.VMEM((4, obs_tiles // 4, 8, LANES), F32),
            pltpu.VMEM((4, obs_tiles // 4, 8, LANES), F32),
            pltpu.VMEM((4, members, columns), F32),
            pltpu.VMEM((8, LANES), F32),
            pltpu.VMEM((8, LANES), F32),
            pltpu.VMEM((near_count, 8, LANES), F32),
            pltpu.VMEM((far_count, 8, LANES), F32),
            pltpu.SemaphoreType.DMA((7,)),
            pltpu.SemaphoreType.DMA,
            pltpu.SemaphoreType.DMA((STEPS, 2, CHUNKS)),
            pltpu.SemaphoreType.DMA((STEPS, 2, CHUNKS)),
            pltpu.SemaphoreType.DMA((3, 4)),
            pltpu.SemaphoreType.DMA((3, 4)),
            pltpu.SemaphoreType.DMA((near_count,)),
            pltpu.SemaphoreType.DMA((near_count,)),
            pltpu.SemaphoreType.DMA((far_count,)),
            pltpu.SemaphoreType.DMA((far_count,)),
        ],
        compiler_params=pltpu.CompilerParams(
            collective_id=0, has_side_effects=True, vmem_limit_bytes=56 * 1024 * 1024
        ),
    )(
        member_group,
        obs_index.reshape(obs_tiles, LANES),
        tracer.reshape(members, rows // 8, 8, tiles, LANES).transpose(0, 1, 3, 2, 4).reshape(-1, LANES),
        coefficients.reshape(4, rows // 8, 8, tiles, LANES).transpose(0, 1, 3, 2, 4).reshape(-1, 8, LANES),
        parameters,
        obs_values,
        obs_variance.reshape(obs_tiles, LANES),
    )
    field = field.reshape(members, rows // 8, tiles, 8, LANES).transpose(0, 1, 3, 2, 4)
    return field.reshape(members, rows, columns), params


def solution(mesh):
    in_specs = (
        P("ens", "slab", None),
        P(None, "slab", None),
        P("ens", None),
        P("slab"),
        P("ens", "slab"),
        P("slab"),
        P(),
    )
    out_specs = (P("ens", "slab", None), P("ens", None))
    return jax.shard_map(local, mesh=mesh, in_specs=in_specs, out_specs=out_specs, check_vma=False)
```

```python
import functools
import math

import jax
import jax.numpy as jnp
from jax import lax
from jax.experimental import pallas as pl
from jax.experimental.pallas import tpu as pltpu
from jax.sharding import PartitionSpec as P

STEPS = 4
GROUPS = 8
LANES = 128
CHUNKS = 2
NEAR = 4
BLOCKS = 16
EDGE = 8
MESH = pl.DeviceIdType.MESH
F32 = jnp.float32
PAIRS = [(a, b) for a in range(4) for b in range(a, 4)]


def lanes_of():
    return lax.broadcasted_iota(jnp.int32, (8, LANES), 1)


def sublanes_of():
    return lax.broadcasted_iota(jnp.int32, (8, LANES), 0)


def parts_of(value):
    high = value.astype(jnp.bfloat16)
    rest = value - high.astype(F32)
    middle = rest.astype(jnp.bfloat16)
    low = (rest - middle.astype(F32)).astype(jnp.bfloat16)
    return jnp.concatenate([high, middle, low], axis=1)


def half_minmod(left, right):
    return 0.5 * jnp.maximum(jnp.minimum(left, right), jnp.minimum(jnp.maximum(left, right), 0.0))


def across_rows(rows, speeds, spreads, bases):
    count = len(rows) - 4
    diffs = [rows[i + 1] - rows[i] for i in range(count + 3)]
    halves = [half_minmod(diffs[i], diffs[i + 1]) for i in range(count + 2)]
    bends = [halves[i + 1] - halves[i] for i in range(count + 1)]
    out = []
    for i in range(count):
        speed = speeds[i]
        change = jnp.where(speed > 0.0, diffs[i + 1] + bends[i], diffs[i + 2] - bends[i + 1])
        out.append(bases[i] - speed * change + spreads[i] * (diffs[i + 2] - diffs[i + 1]))
    return out


def kernel(
    slabs,
    tiles,
    group_ref,
    index_ref,
    tracer_ref,
    coef_ref,
    params_ref,
    values_ref,
    variance_ref,
    field_out,
    params_out,
    tracer_v,
    coef_v,
    own_params,
    variance_v,
    index_v,
    place_v,
    place,
    spread_out,
    pick_out,
    params_t,
    coef_x,
    cells,
    halo,
    slopes,
    partial_c,
    final_c,
    mask_v,
    found,
    field_v,
    all_params,
    all_values,
    picked,
    all_picked,
    moved,
    part_near,
    part_far,
    sums_near,
    sums_far,
    load_sem,
    out_sem,
    halo_send,
    halo_recv,
    ens_send,
    ens_recv,
    near_send,
    near_recv,
    far_send,
    far_recv,
):
    ens = lax.axis_index("ens")
    slab = lax.axis_index("slab")
    rows = 16
    segment = tiles * LANES // BLOCKS
    halves = segment // LANES
    per_chunk = segment // CHUNKS
    groups = per_chunk // 8
    far_count = slabs // NEAR
    near_count = 4 * NEAR
    quarter = picked.shape[1]
    obs_tiles = 4 * quarter
    has_left = slab > 0
    has_right = slab < slabs - 1
    near_me = ens * NEAR + lax.rem(slab, NEAR)
    far_me = slab // NEAR
    lane = lanes_of()
    sub = sublanes_of()

    def near_device(i):
        return (i // NEAR, far_me * NEAR + lax.rem(i, NEAR))

    def far_device(i):
        return (ens, i * NEAR + lax.rem(slab, NEAR))

    loads = [
        pltpu.make_async_copy(tracer_ref, tracer_v, load_sem.at[0]),
        pltpu.make_async_copy(coef_ref, coef_v, load_sem.at[1]),
        pltpu.make_async_copy(params_ref, own_params, load_sem.at[2]),
        pltpu.make_async_copy(variance_ref, variance_v, load_sem.at[3]),
        pltpu.make_async_copy(
            values_ref.at[:, pl.ds(pl.multiple_of(ens * (quarter * LANES), LANES), quarter * LANES)],
            all_values.at[ens],
            load_sem.at[4],
        ),
        pltpu.make_async_copy(index_ref, index_v, load_sem.at[5]),
    ]
    for load in loads:
        load.start()

    barrier = pltpu.get_barrier_semaphore()

    @pl.loop(1, near_count)
    def _(p):
        pl.semaphore_signal(
            barrier, inc=1, device_id=near_device(lax.rem(near_me + p, near_count)), device_id_type=MESH
        )

    @pl.loop(1, far_count)
    def _(p):
        pl.semaphore_signal(
            barrier, inc=1, device_id=far_device(lax.rem(far_me + p, far_count)), device_id_type=MESH
        )

    @pl.when(has_left)
    def _():
        pl.semaphore_signal(barrier, inc=1, device_id=(ens, slab - 1), device_id_type=MESH)

    @pl.when(has_right)
    def _():
        pl.semaphore_signal(barrier, inc=1, device_id=(ens, slab + 1), device_id_type=MESH)

    loads[0].wait()

    def of_tile(row, j):
        return (row // 8 * tiles + j) * 8 + lax.rem(row, 8)

    def take_row(row):
        for h in range(halves):
            block = [
                tracer_v[pl.ds(of_tile(row, b * halves + h), 8, stride=rows * tiles), :]
                for b in range(BLOCKS)
            ]
            cells[0, row, pl.ds(EDGE + h * LANES, LANES), :] = jnp.transpose(jnp.concatenate(block, axis=0))

    def edge_row(i):
        return i + i // 2 * (rows - 4)

    @pl.loop(0, 4)
    def _(i):
        take_row(edge_row(i))

    zero = jnp.zeros((8, LANES), F32)

    def clear(side):
        @pl.loop(0, STEPS)
        def _(t):
            for r in range(2):
                for i in range(segment // 8):
                    halo[t, side, r, pl.ds(i * 8, 8), :] = zero

    pl.when(jnp.logical_not(has_left))(functools.partial(clear, 0))
    pl.when(jnp.logical_not(has_right))(functools.partial(clear, 1))

    neighbours = jnp.where(has_left, 1, 0) + jnp.where(has_right, 1, 0)
    pl.semaphore_wait(barrier, near_count + far_count - 2 + neighbours)

    def halo_copy(t, side, k):
        start = pl.multiple_of(k * per_chunk, per_chunk)
        return pltpu.make_async_remote_copy(
            src_ref=cells.at[
                t,
                pl.ds(rows - 2, 2) if side == 0 else pl.ds(0, 2),
                pl.ds(pl.multiple_of(EDGE + start, 8), per_chunk),
            ],
            dst_ref=halo.at[t, side, :, pl.ds(start, per_chunk)],
            send_sem=halo_send.at[t, side, k],
            recv_sem=halo_recv.at[t, side, k],
            device_id=(ens, slab + 1 if side == 0 else slab - 1),
            device_id_type=MESH,
        )

    def send_halo(t, side, k):
        @pl.when(has_right if side == 0 else has_left)
        def _():
            halo_copy(t, side, k).start()

    def wait_halo(t, side, k):
        @pl.when(has_left if side == 0 else has_right)
        def _():
            halo_copy(t, side, k).wait_recv()

    @pl.loop(0, CHUNKS)
    def _(k):
        send_halo(0, 0, k)
        send_halo(0, 1, k)

    loads[2].wait()

    def params_copy(p):
        return pltpu.make_async_remote_copy(
            src_ref=own_params,
            dst_ref=all_params.at[ens],
            send_sem=ens_send.at[0, p],
            recv_sem=ens_recv.at[0, p],
            device_id=(lax.rem(ens + p, 4), slab),
            device_id_type=MESH,
        )

    def values_copy(p):
        target = lax.rem(ens + p, 4)
        return pltpu.make_async_remote_copy(
            src_ref=values_ref.at[:, pl.ds(pl.multiple_of(target * (quarter * LANES), LANES), quarter * LANES)],
            dst_ref=all_values.at[ens],
            send_sem=ens_send.at[1, p],
            recv_sem=ens_recv.at[1, p],
            device_id=(target, slab),
            device_id_type=MESH,
        )

    def picked_copy(p):
        target = lax.rem(ens + p, 4)
        return pltpu.make_async_remote_copy(
            src_ref=picked.at[target],
            dst_ref=all_picked.at[ens],
            send_sem=ens_send.at[2, p],
            recv_sem=ens_recv.at[2, p],
            device_id=(target, slab),
            device_id_type=MESH,
        )

    for p in range(1, 4):
        params_copy(p).start()
        values_copy(p).start()

    from_lane = lax.broadcasted_iota(jnp.int32, (3 * LANES, LANES), 0)
    to_lane = lax.broadcasted_iota(jnp.int32, (3 * LANES, LANES), 1)
    same_block = ((from_lane >> 3) & (BLOCKS - 1)) == (to_lane >> 3)
    for r in range(8):
        spread_out[:, pl.ds(r * LANES, LANES)] = jnp.where(
            same_block & ((from_lane & 7) == r), 1.0, 0.0
        ).astype(jnp.bfloat16)
    for i in range(quarter):
        pick_out[pl.ds(i * 3 * LANES, 3 * LANES), :] = jnp.where(
            ((from_lane & 7) == (to_lane & 7)) & ((to_lane >> 3) == i), 1.0, 0.0
        ).astype(jnp.bfloat16)

    @pl.loop(2, rows - 2)
    def _(row):
        take_row(row)

    for h in range(halves):
        block = [own_params[:, pl.ds((b * halves + h) * LANES, LANES)] for b in range(BLOCKS)]
        params_t[pl.ds(h * LANES, LANES), :] = jnp.transpose(jnp.concatenate(block, axis=0))

    loads[1].wait()

    def expand(c, eight, h, scale):
        block = [coef_v[(c * 2 + eight) * tiles + b * halves + h] for b in range(BLOCKS)]
        turned = jnp.transpose(jnp.concatenate(block, axis=0))
        wide = jnp.dot(parts_of(turned), spread_out[...], preferred_element_type=F32)
        window = pl.ds(pl.multiple_of(h * LANES, LANES), LANES)
        for r in range(8):
            value = wide[:, r * LANES : (r + 1) * LANES]
            if scale:
                value = value * params_t[window, :]
            coef_x[c, eight * 8 + r, window, :] = value

    @pl.loop(0, 3 * 2 * halves)
    def _(n):
        expand(n // (2 * halves), lax.rem(n // halves, 2), lax.rem(n, halves), False)

    @pl.loop(0, 2 * halves)
    def _(n):
        expand(3, n // halves, lax.rem(n, halves), True)

    def wrap_row(t, r):
        cells[t, r, pl.ds(0, 8), :] = pltpu.roll(cells[t, r, pl.ds(EDGE + segment - 8, 8), :], 8, 1)
        cells[t, r, pl.ds(EDGE + segment, 8), :] = pltpu.roll(cells[t, r, pl.ds(EDGE, 8), :], LANES - 8, 1)

    def along_columns(t, rows_here, k):
        start = k * per_chunk
        for s, r in enumerate(rows_here):
            for i in range(groups + 1):
                at = start + (EDGE - 1 + i * 8)
                before, here, after = [cells[t, r, pl.ds(at + d, 8), :] for d in (-1, 0, 1)]
                slopes[s, pl.ds(i * 8, 8), :] = half_minmod(here - before, after - here)
        for s, r in enumerate(rows_here):
            for i in range(groups):
                at = start + (EDGE + i * 8)
                window = pl.ds(pl.multiple_of(start + i * 8, 8), 8)
                before, here, after = [cells[t, r, pl.ds(at + d, 8), :] for d in (-1, 0, 1)]
                half_before, half, half_after = [slopes[s, pl.ds(i * 8 + d, 8), :] for d in (0, 1, 2)]
                down, up = here - before, after - here
                forward = down + (half - half_before)
                backward = up - (half_after - half)
                speed = coef_x[1, r, window, :]
                partial_c[r, window, :] = (
                    here
                    - speed * jnp.where(speed > 0.0, forward, backward)
                    + coef_x[2, r, window, :] * (up - down)
                    + coef_x[3, r, window, :]
                )

    def finish_rows(t, first, last, i, before, after, store):
        window = pl.ds(pl.multiple_of(i * 8, 8), 8)
        inner = pl.ds(pl.multiple_of(EDGE + i * 8, 8), 8)
        taken = (
            [halo[t, 0, r, window, :] for r in range(before)]
            + [cells[t, r, inner, :] for r in range(max(first - 2, 0), min(last + 2, rows))]
            + [halo[t, 1, r, window, :] for r in range(after)]
        )
        new = across_rows(
            taken,
            [coef_x[0, r, window, :] for r in range(first, last)],
            [coef_x[2, r, window, :] for r in range(first, last)],
            [partial_c[r, window, :] for r in range(first, last)],
        )
        for r, value in zip(range(first, last), new):
            store(r, i, value)

    def one_step(t, final):
        def store(r, i, value):
            if final:
                final_c[pl.ds(pl.multiple_of(r * segment + i * 8, 8), 8), :] = value
            else:
                cells[t + 1, r, pl.ds(pl.multiple_of(EDGE + i * 8, 8), 8), :] = value

        for r in range(rows):
            wrap_row(t, r)

        def edges(k):
            along_columns(t, (0, 1), k)
            along_columns(t, (rows - 2, rows - 1), k)
            for side in range(2):
                wait_halo(t, side, k)
                first = (rows - 2) * side

                @pl.loop(0, groups, step=4)
                def _(i):
                    for u in range(4):
                        finish_rows(
                            t, first, first + 2, k * groups + i + u, 2 - 2 * side, 2 * side, store
                        )

                if not final:
                    send_halo(t + 1, 1 - side, k)

        def inside(k):
            @pl.loop(2, rows - 2, step=2)
            def _(r):
                along_columns(t, (r, r + 1), k)

            @pl.loop(0, groups)
            def _(i):
                finish_rows(t, 2, rows - 2, k * groups + i, 0, 0, store)

        @pl.loop(0, CHUNKS)
        def _(k):
            pl.when(k == CHUNKS - 1)(lambda: inside(k))
            edges(k)
            pl.when(k < CHUNKS - 1)(lambda: inside(k))

    @pl.loop(0, STEPS - 1)
    def _(t):
        one_step(t, False)

    members = 32
    group_row = jnp.zeros((8, LANES), jnp.int32) - 1
    for m in range(members):
        group_row = jnp.where(lane == m, group_ref[m], group_row)
    slot_row = jnp.zeros((8, LANES), jnp.int32)
    for m in range(members):
        slot_row = slot_row + jnp.where((group_row == group_ref[m]) & (lane > m), 1, 0)
    group_own = jnp.zeros((8, LANES), jnp.int32)
    for i in range(8):
        group_own = jnp.where(sub == i, group_ref[ens * 8 + i], group_own)
    slot_own = jnp.zeros((8, LANES), jnp.int32)
    for m in range(members):
        slot_own = slot_own + jnp.where((group_own == group_ref[m]) & (sub + ens * 8 > m), 1, 0)
    in_slot = [jnp.where(slot_row == s, 1.0, 0.0) for s in range(4)]
    by_group = jnp.concatenate(
        [jnp.where(group_row == sub, in_slot[s], 0.0) for s in range(4)], axis=0
    )[:, :members]
    by_own = jnp.concatenate(
        [jnp.where(group_row == group_own, in_slot[s], 0.0) for s in range(4)], axis=0
    )[:, :members]

    def pick(chosen, held):
        return jnp.dot(chosen, held, precision=lax.Precision.HIGHEST, preferred_element_type=F32)

    spread_of = 1.0 / math.sqrt(3.0)

    def centred(four):
        mean = (four[0] + four[1] + four[2] + four[3]) * 0.25
        return [(x - mean) * spread_of for x in four]

    all_params[ens] = own_params[...]
    for p in range(1, 4):
        params_copy(p).wait_recv()
    columns = tiles * LANES
    piece = min(512, columns)

    @pl.loop(0, columns // piece)
    def _(c):
        window = pl.ds(pl.multiple_of(c * piece, piece), piece)
        held = jnp.concatenate([all_params[q, :, window] for q in range(4)], axis=0)
        ordered = pick(by_own, held)
        for s, value in enumerate(centred([ordered[s * 8 : s * 8 + 8] for s in range(4)])):
            moved[s, :, window] = value

    loads[3].wait()
    loads[4].wait()
    for p in range(1, 4):
        values_copy(p).wait_recv()
    ordered_values = pick(by_group, jnp.concatenate([all_values[q] for q in range(4)], axis=0))
    total_obs = float(obs_tiles * LANES * slabs)
    weights = [
        jnp.broadcast_to(1.0 / (variance_v[pl.ds(ens * quarter + i, 1), :] * total_obs), (8, LANES))
        for i in range(quarter)
    ]
    weight = jnp.concatenate(weights, axis=1)

    loads[5].wait()
    cell = index_v[...]
    column_of = cell & (tiles * LANES - 1)
    place_v[...] = cell // (tiles * LANES) * segment + (column_of & (segment - 1))
    to_smem = pltpu.make_async_copy(place_v, place, load_sem.at[6])
    to_smem.start()
    block_of = jnp.transpose((column_of // segment).astype(F32))
    lane_block = (lax.broadcasted_iota(jnp.int32, (LANES, LANES), 1) >> 3).astype(F32)
    for i in range(obs_tiles):
        mask_v[i] = jnp.where(
            jnp.broadcast_to(block_of[:, i : i + 1], (LANES, LANES)) == lane_block, 1.0, 0.0
        )
    to_smem.wait()

    one_step(STEPS - 1, True)

    def gather_quarter(q):
        @pl.loop(0, quarter)
        def _(i):
            tile = q * quarter + i
            for g in range(LANES // 8):
                taken = jnp.zeros((8, LANES), F32)
                for u in range(8):
                    row = final_c[pl.ds(place[tile, g * 8 + u], 1), :]
                    taken = jnp.where(sub == u, jnp.broadcast_to(row, (8, LANES)), taken)
                window = pl.ds(pl.multiple_of(i * LANES + g * 8, 8), 8)
                found[window, :] = taken * mask_v[tile, pl.ds(g * 8, 8), :]

        parts = [parts_of(found[pl.ds(i * LANES, LANES), :]) for i in range(quarter)]
        total = jnp.dot(jnp.concatenate(parts, axis=1), pick_out[...], preferred_element_type=F32)
        turned = jnp.transpose(total)
        for i in range(quarter):
            picked[q, i] = turned[i * 8 : i * 8 + 8]

    def emit_rows(first, last):
        @pl.loop(first, last)
        def _(r):
            for h in range(halves):
                start = pl.multiple_of(r * segment + h * LANES, LANES)
                turned = jnp.transpose(final_c[pl.ds(start, LANES), :])
                for b in range(BLOCKS):
                    field_v[pl.ds(of_tile(r, b * halves + h), 8, stride=rows * tiles), :] = turned[
                        b * 8 : b * 8 + 8
                    ]

    @pl.loop(1, 5)
    def _(p):
        gather_quarter(lax.rem(ens + p, 4))
        pl.when(p < 4)(lambda: picked_copy(p).start())

    for i in range(quarter):
        all_picked[ens, i] = picked[ens, i]
    emit_rows(0, 6)
    for p in range(1, 4):
        picked_copy(p).wait_recv()

    held = jnp.concatenate(
        [
            jnp.concatenate([all_picked[q, i] for i in range(quarter)], axis=1)
            for q in range(4)
        ],
        axis=0,
    )
    ordered = pick(by_group, held)
    ordered = [ordered[s * 8 : s * 8 + 8] for s in range(4)]
    innovation = [
        (ordered_values[s * 8 : s * 8 + 8] - ordered[s]) * weight for s in range(4)
    ]
    anomalies = centred(ordered)
    weighted = [a * weight for a in anomalies]
    products = [(weighted[a], anomalies[b]) for a, b in PAIRS] + [
        (anomalies[a], innovation[b]) for a in range(4) for b in range(4)
    ]
    packed = jnp.zeros((8, LANES), F32)
    for position, (left, right) in enumerate(products):
        both = left * right
        folded = both[:, :LANES]
        for i in range(1, quarter):
            folded = folded + both[:, i * LANES : (i + 1) * LANES]
        packed = jnp.where(lane == position, jnp.sum(folded, axis=1, keepdims=True), packed)

    def sum_over(value, part, sums, me, count, device, send, recv, meanwhile):
        part[...] = value

        def copy(i, slot):
            return pltpu.make_async_remote_copy(
                src_ref=part,
                dst_ref=sums.at[me],
                send_sem=send.at[slot],
                recv_sem=recv.at[slot],
                device_id=device(i),
                device_id_type=MESH,
            )

        copies = [copy(lax.rem(me + p, count), p) for p in range(1, count)]
        for one in copies:
            one.start()
        sums[me] = value
        meanwhile()
        for one in copies:
            one.wait()
        total = sums[0]
        for i in range(1, count):
            total = total + sums[i]
        return total

    field_store = pltpu.make_async_copy(field_v, field_out, out_sem)

    def rest_of_field():
        emit_rows(11, rows)
        field_store.start()
        for p in range(1, 4):
            params_copy(p).wait_send()
            values_copy(p).wait_send()
            picked_copy(p).wait_send()

        @pl.loop(0, STEPS)
        def _(t):
            @pl.loop(0, CHUNKS)
            def _(k):
                @pl.when(has_right)
                def _():
                    halo_copy(t, 0, k).wait_send()

                @pl.when(has_left)
                def _():
                    halo_copy(t, 1, k).wait_send()

    total = sum_over(
        packed,
        part_near,
        sums_near,
        near_me,
        near_count,
        near_device,
        near_send,
        near_recv,
        lambda: emit_rows(6, 11),
    )
    total = sum_over(
        total, part_far, sums_far, far_me, far_count, far_device, far_send, far_recv, rest_of_field
    )

    mine = jnp.zeros((8, LANES), F32)
    for g in range(GROUPS):
        mine = jnp.where(group_own == g, jnp.broadcast_to(total[g : g + 1], (8, LANES)), mine)

    def column(i):
        return jnp.broadcast_to(mine[:, i : i + 1], (8, LANES))

    a = {}
    for i, (p, q) in enumerate(PAIRS):
        a[p, q] = column(i) + (1.0 if p == q else 0.0)
    b = []
    for p in range(4):
        value = column(len(PAIRS) + p * 4)
        for q in range(1, 4):
            value = jnp.where(slot_own == q, column(len(PAIRS) + p * 4 + q), value)
        b.append(value)
    low = {}
    for p in range(4):
        for q in range(p + 1, 4):
            low[q, p] = a[p, q] / a[p, p]
        for q in range(p + 1, 4):
            for r in range(q, 4):
                a[q, r] = a[q, r] - low[q, p] * a[p, r]
    for p in range(4):
        for q in range(p + 1, 4):
            b[q] = b[q] - low[q, p] * b[p]
    solved = [b[p] / a[p, p] for p in range(4)]
    for p in range(2, -1, -1):
        for q in range(p + 1, 4):
            solved[p] = solved[p] - low[q, p] * solved[q]

    for j in range(tiles):
        window = pl.ds(j * LANES, LANES)
        value = own_params[:, window]
        for s in range(4):
            value = value + solved[s] * moved[s, :, window]
        params_out[:, window] = value

    field_store.wait()


def local(tracer, coefficients, parameters, obs_index, obs_values, obs_variance, member_group):
    members, rows, columns = tracer.shape
    slabs = lax.axis_size("slab")
    tiles = columns // LANES
    obs_tiles = obs_index.shape[0] // LANES
    far_count = slabs // NEAR
    near_count = 4 * NEAR
    segment = columns // BLOCKS
    wide = (rows, segment, LANES)
    smem = pl.BlockSpec(memory_space=pltpu.SMEM)
    anywhere = pl.BlockSpec(memory_space=pl.ANY)
    vmem = pl.BlockSpec(memory_space=pltpu.VMEM)
    field, params = pl.pallas_call(
        functools.partial(kernel, slabs, tiles),
        out_shape=(
            jax.ShapeDtypeStruct((members * rows * tiles, LANES), F32),
            jax.ShapeDtypeStruct((members, columns), F32),
        ),
        in_specs=[smem] + [pl.BlockSpec(memory_space=pltpu.HBM)] * 6,
        out_specs=(anywhere, vmem),
        scratch_shapes=[
            pltpu.VMEM((members * rows * tiles, LANES), F32),
            pltpu.VMEM((4 * rows // 8 * tiles, 8, LANES), F32),
            pltpu.VMEM((members, columns), F32),
            pltpu.VMEM((obs_tiles, LANES), F32),
            pltpu.VMEM((obs_tiles, LANES), jnp.int32),
            pltpu.VMEM((obs_tiles, LANES), jnp.int32),
            pltpu.SMEM((obs_tiles, LANES), jnp.int32),
            pltpu.VMEM((3 * LANES, 8 * LANES), jnp.bfloat16),
            pltpu.VMEM((obs_tiles // 4 * 3 * LANES, LANES), jnp.bfloat16),
            pltpu.VMEM((segment, LANES), F32),
            pltpu.VMEM((4,) + wide, F32),
            pltpu.VMEM((STEPS, rows, segment + 2 * EDGE, LANES), F32),
            pltpu.VMEM((STEPS, 2, 2, segment, LANES), F32),
            pltpu.VMEM((2, segment // CHUNKS + 8, LANES), F32),
            pltpu.VMEM(wide, F32),
            pltpu.VMEM((rows * segment, LANES), F32),
            pltpu.VMEM((obs_tiles, LANES, LANES), F32),
            pltpu.VMEM((obs_tiles // 4 * LANES, LANES), F32),
            pltpu.VMEM((members * rows * tiles, LANES), F32),
            pltpu.VMEM((4, members, columns), F32),
            pltpu.VMEM((4, members, obs_tiles // 4 * LANES), F32),
            pltpu.VMEM((4, obs_tiles // 4, 8, LANES), F32),
            pltpu.VMEM((4, obs_tiles // 4, 8, LANES), F32),
            pltpu.VMEM((4, members, columns), F32),
            pltpu.VMEM((8, LANES), F32),
            pltpu.VMEM((8, LANES), F32),
            pltpu.VMEM((near_count, 8, LANES), F32),
            pltpu.VMEM((far_count, 8, LANES), F32),
            pltpu.SemaphoreType.DMA((7,)),
            pltpu.SemaphoreType.DMA,
            pltpu.SemaphoreType.DMA((STEPS, 2, CHUNKS)),
            pltpu.SemaphoreType.DMA((STEPS, 2, CHUNKS)),
            pltpu.SemaphoreType.DMA((3, 4)),
            pltpu.SemaphoreType.DMA((3, 4)),
            pltpu.SemaphoreType.DMA((near_count,)),
            pltpu.SemaphoreType.DMA((near_count,)),
            pltpu.SemaphoreType.DMA((far_count,)),
            pltpu.SemaphoreType.DMA((far_count,)),
        ],
        compiler_params=pltpu.CompilerParams(
            collective_id=0, has_side_effects=True, vmem_limit_bytes=56 * 1024 * 1024
        ),
    )(
        member_group,
        obs_index.reshape(obs_tiles, LANES),
        tracer.reshape(members, rows // 8, 8, tiles, LANES).transpose(0, 1, 3, 2, 4).reshape(-1, LANES),
        coefficients.reshape(4, rows // 8, 8, tiles, LANES).transpose(0, 1, 3, 2, 4).reshape(-1, 8, LANES),
        parameters,
        obs_values,
        obs_variance.reshape(obs_tiles, LANES),
    )
    field = field.reshape(members, rows // 8, tiles, 8, LANES).transpose(0, 1, 3, 2, 4)
    return field.reshape(members, rows, columns), params


def solution(mesh):
    in_specs = (
        P("ens", "slab", None),
        P(None, "slab", None),
        P("ens", None),
        P("slab"),
        P("ens", "slab"),
        P("slab"),
        P(),
    )
    out_specs = (P("ens", "slab", None), P("ens", None))
    return jax.shard_map(local, mesh=mesh, in_specs=in_specs, out_specs=out_specs, check_vma=False)
```
